32 devices in a mesh: slab: 8 (over z, y), head: 4 (over x, core).
Axes of the slice: x: 2, y: 2, z: 4, core: 2. Of those that a mesh axis runs over, the one named last changes fastest.
Arguments:
- tokens: bfloat16 [16384, 384], P(('slab', 'head')), may hold values from -6 to 6
- norm_gain: float32 [384], replicated, may hold values from 0.25 to 1.75
- w_qkv: bfloat16 [3, 384, 384], replicated, may hold values from -0.3125 to 0.3125
- w_out: bfloat16 [384, 384], replicated, may hold values from -0.625 to 0.625
- cotangent: bfloat16 [16384, 384], P(('slab', 'head')), may hold values from -6 to 6
- neighbours: int32 [128, 8], P('slab'), may hold values from 0 to 127, as said below
- counts: int32 [128], P('slab'), may hold values from 2 to 8, as said below
Outputs:
- output: bfloat16 [16384, 384], P(('slab', 'head'))
- d_tokens: bfloat16 [16384, 384], P(('slab', 'head'))
- d_w_qkv: float32 [3, 384, 384], P(None, None, 'head')
- d_w_out: float32 [384, 384], replicated
- d_gain: float32 [384], replicated
The draws below stay inside these ranges and needn't reach their ends.
Inputs may be any that keep to these rules, and one draw needn't show every extreme that they name: `neighbours`: entry 0 of block b's list is b itself; the entries of a list are distinct and each lies within 16 blocks of b along the periodic block order (modulo 128); every block lists one block at distance exactly 16. Only the first counts[b] slots of block b's list are live; the first block of every slab has all 8 live.
All inputs are finite; a program needn't handle non-finite values.
Results may differ from the reference program's by a relative error of at most 0.024.
Values may be sent and summed in bfloat16 or wider, within the bound.
A program may use at most 192 MiB of HBM per device.

```python
import math
import jax
import jax.numpy as jnp
from jax import lax

D = 384
HEADS = 12
BLK = 128
NNB = 8
REACH = 16
SLAB_BLK = 16
HD = 32
NBLK = 128
TOKENS = 16384


def draw_neighbours(key, part):
    blocks = jnp.arange(NBLK, dtype=jnp.int32)
    offsets_pool = jnp.concatenate([jnp.arange(1 - REACH, 0, dtype=jnp.int32), jnp.arange(1, REACH, dtype=jnp.int32)])
    pool_size = 2 * REACH - 2
    raw_affinity = jax.random.randint(jax.random.fold_in(key, 11), (NBLK, pool_size), 0, 2 ** 20) * pool_size + jnp.arange(pool_size, dtype=jnp.int32)[None, :]
    ranking = jnp.argsort(raw_affinity, axis=1, stable=True)
    picked = offsets_pool[ranking[:, :NNB - 2]]
    farthest = jnp.where(blocks % 2 == 0, REACH, -REACH).astype(jnp.int32)
    offsets = jnp.concatenate([jnp.zeros((NBLK, 1), jnp.int32), farthest[:, None], picked], 1)
    return ((blocks[:, None] + offsets) % NBLK).astype(jnp.int32)


def draw_counts(key, part):
    n_slabs = NBLK // SLAB_BLK
    density = jax.random.randint(jax.random.fold_in(key, 21), (n_slabs,), 2, NNB + 1)
    jitter = jax.random.randint(jax.random.fold_in(key, 22), (NBLK,), -1, 2)
    counts = jnp.clip(jnp.repeat(density, SLAB_BLK, total_repeat_length=NBLK) + jitter, 2, NNB)
    leading = jnp.arange(NBLK, dtype=jnp.int32) % SLAB_BLK == 0
    return jnp.where(leading, NNB, counts).astype(jnp.int32)


def levels(rng, dims, split, low, largest):
    gain, own = 1.0, jax.random.fold_in(rng, 6)
    for axis_at, parts in split:
        draws = jnp.exp(jax.random.uniform(jax.random.fold_in(own, axis_at), (parts,), jnp.float32, low / len(split), largest / len(split)))
        gain = gain * jnp.repeat(draws, dims[axis_at] // parts).reshape([-1 if axis == axis_at else 1 for axis in range(len(dims))])
    return gain


def centred(own_key, shape, scale, reach, cuts=(), kind=jnp.bfloat16):
    drawn = scale * jax.random.normal(own_key, shape, jnp.float32)
    if cuts:
        drawn = drawn * levels(own_key, shape, cuts, -0.22, 0.18)
    return jnp.clip(drawn, -reach, reach).astype(kind)


def setup_inputs(seed: int = 0) -> dict:
    streams_of = jax.random.split(jax.random.key(seed), 8)
    return {
        "tokens": centred(streams_of[0], (TOKENS, D), 1.0, 6.0, ((0, 32),)),
        "norm_gain": jnp.clip(1.0 + 0.15 * jax.random.normal(streams_of[1], (D,), jnp.float32), 0.25, 1.75),
        "w_qkv": centred(streams_of[2], (3, D, D), D ** -0.5, 0.3125),
        "w_out": centred(streams_of[3], (D, D), (D // 4) ** -0.5, 0.625),
        "cotangent": centred(streams_of[4], (TOKENS, D), 1.0, 6.0, ((0, 32),)),
        "neighbours": draw_neighbours(jax.random.fold_in(streams_of[7], 71), 0),
        "counts": draw_counts(jax.random.fold_in(streams_of[7], 71), 0),
    }


exponent_divisor = 10.0
norm_eps = 1e-06

def normalize(projected, head_dim):
    by_head = projected.reshape(projected.shape[:-1] + (projected.shape[-1] // head_dim, head_dim))
    length = jnp.sqrt(lax.optimization_barrier(jnp.sum(by_head * by_head, -1, keepdims=True)))
    divisor = jnp.maximum(length, 0.7 * math.sqrt(head_dim))
    return (by_head / divisor, divisor, length > 0.7 * math.sqrt(head_dim))

def unit_heads(projected, head_dim):
    unit, divisor, active = normalize(projected, head_dim)
    return unit.reshape(projected.shape)

def norm_back(projected, grad, head_dim):
    unit, divisor, active = normalize(projected, head_dim)
    along = grad.astype(jnp.float32).reshape(unit.shape)
    inner = lax.optimization_barrier(jnp.sum(unit * along, -1, keepdims=True))
    result = (along - jnp.where(active, unit * inner, 0.0)) / divisor
    return result.reshape(projected.shape)

def attention_weights(asking_matrix, lookup_matrix, counts):
    slot_ids = jnp.arange(lookup_matrix.shape[1], dtype=jnp.int32) // asking_matrix.shape[1]
    raw_affinity = exponent_divisor * jnp.einsum('pcxt,pqxt->pxcq', asking_matrix.astype(jnp.float32), lookup_matrix.astype(jnp.float32))
    live_mask = (slot_ids[None, :] < counts[:, None]).astype(jnp.float32)
    raised = jnp.exp(raw_affinity) * live_mask[:, None, None, :]
    return raised / lax.optimization_barrier(jnp.sum(raised, -1, keepdims=True))

def reference(tokens, norm_gain, w_qkv, w_out, cotangent, neighbours, counts):
    tok_f32 = tokens.astype(jnp.float32)
    inverse = lax.rsqrt(lax.optimization_barrier(jnp.mean(tok_f32 * tok_f32, -1, keepdims=True)) + norm_eps)
    normed = (tok_f32 * inverse * norm_gain).astype(jnp.bfloat16)
    projected = jnp.stack([jnp.dot(normed, w_qkv[c], preferred_element_type=jnp.float32) for c in range(3)])
    q_heads = unit_heads(projected[0], HD).astype(jnp.bfloat16)
    k_heads = unit_heads(projected[1], HD).astype(jnp.bfloat16)
    v_heads = projected[2].astype(jnp.bfloat16)
    group_size = 8 if SLAB_BLK % 8 == 0 else SLAB_BLK
    n_groups = NBLK // group_size
    key_blocks = jnp.stack([k_heads, v_heads]).reshape(2, NBLK, BLK, HEADS, HD)
    query_groups = q_heads.reshape(n_groups, group_size, BLK, HEADS, HD)
    lookup_groups = neighbours.reshape(n_groups, group_size, NNB)
    count_groups = counts.reshape(n_groups, group_size)

    def fetch(lookup_rows):
        both = key_blocks[:, lookup_rows.reshape(-1)]
        return both.reshape(2, group_size, NNB * BLK, HEADS, HD)

    def attend(inputs):
        asking_matrix, lookup_rows, live = inputs
        both = fetch(lookup_rows)
        weights_bf = attention_weights(asking_matrix, both[0], live).astype(jnp.bfloat16)
        result = jnp.einsum('ghqk,gkhd->gqhd', weights_bf.astype(jnp.float32), both[1].astype(jnp.float32))
        return result.astype(jnp.bfloat16)
    attended = lax.map(attend, (query_groups, lookup_groups, count_groups)).reshape(TOKENS, D)
    output = (tok_f32 + jnp.dot(attended, w_out, preferred_element_type=jnp.float32)).astype(jnp.bfloat16)
    d_w_out = jnp.dot(attended.T, cotangent, preferred_element_type=jnp.float32)
    d_attended = jnp.dot(cotangent, w_out.T, preferred_element_type=jnp.float32).astype(jnp.bfloat16)
    d_groups = d_attended.reshape(n_groups, group_size, BLK, HEADS, HD)

    def backward_group(grad_buffer, inputs):
        asking_matrix, d_attn, lookup_rows, live = inputs
        both = fetch(lookup_rows)
        normalized_affinity = attention_weights(asking_matrix, both[0], live)
        weights_bf = normalized_affinity.astype(jnp.bfloat16)
        affinity_share_cotangent = jnp.einsum('pcxt,pqxt->pxcq', d_attn.astype(jnp.float32), both[1].astype(jnp.float32))
        pairwise_dot_sum = lax.optimization_barrier(jnp.sum(affinity_share_cotangent * normalized_affinity, -1, keepdims=True))
        affinity_cotangent = (exponent_divisor * normalized_affinity * (affinity_share_cotangent - pairwise_dot_sum)).astype(jnp.bfloat16).astype(jnp.float32)
        d_query = jnp.einsum('ghqk,gkhd->gqhd', affinity_cotangent, both[0].astype(jnp.float32))
        d_keys = jnp.einsum('ghqk,gqhd->gkhd', affinity_cotangent, asking_matrix.astype(jnp.float32))
        d_values = jnp.einsum('ghqk,gqhd->gkhd', weights_bf.astype(jnp.float32), d_attn.astype(jnp.float32))
        stacked = jnp.stack([d_keys, d_values]).reshape(2, group_size * NNB, BLK, HEADS, HD)
        grad_buffer = grad_buffer.at[:, lookup_rows.reshape(-1)].add(stacked)
        return (grad_buffer, d_query)
    start_buffer = jnp.zeros((2, NBLK, BLK, HEADS, HD), jnp.float32)
    grad_buffer, d_query_groups = lax.scan(backward_group, start_buffer, (query_groups, d_groups, lookup_groups, count_groups))
    dq_heads = d_query_groups.reshape(TOKENS, D).astype(jnp.bfloat16)
    dk_heads = grad_buffer[0].reshape(TOKENS, D).astype(jnp.bfloat16)
    dv_heads = grad_buffer[1].reshape(TOKENS, D).astype(jnp.bfloat16)
    d_q = norm_back(projected[0], dq_heads, HD).astype(jnp.bfloat16)
    d_k = norm_back(projected[1], dk_heads, HD).astype(jnp.bfloat16)
    d_qkv = [d_q, d_k, dv_heads]
    d_normed = jnp.dot(d_qkv[0], w_qkv[0].T, preferred_element_type=jnp.float32)
    d_normed = d_normed + jnp.dot(d_qkv[1], w_qkv[1].T, preferred_element_type=jnp.float32)
    d_normed = d_normed + jnp.dot(d_qkv[2], w_qkv[2].T, preferred_element_type=jnp.float32)
    d_w_qkv = jnp.stack([jnp.dot(normed.T, d_qkv[c], preferred_element_type=jnp.float32) for c in range(3)])
    d_gain = lax.optimization_barrier(jnp.sum(d_normed * tok_f32 * inverse, 0))
    scaled = d_normed * norm_gain
    d_tokens = cotangent.astype(jnp.float32) + inverse * scaled - tok_f32 * inverse ** 3 * lax.optimization_barrier(jnp.mean(scaled * tok_f32, -1, keepdims=True))
    return (output, d_tokens.astype(jnp.bfloat16), d_w_qkv, d_w_out, d_gain)
```

```python
import functools
import math

import jax
import jax.numpy as jnp
from jax import lax
from jax.experimental import pallas as pl
from jax.experimental.pallas import tpu as pltpu
from jax.sharding import PartitionSpec as P

HEADS = 12
BLK = 128
REACH = 16
MESH = pl.DeviceIdType.MESH
F32, BF16 = jnp.float32, jnp.bfloat16

SCORE_SCALE = 10.0
LOG2E = 1.0 / math.log(2.0)
norm_eps = 1e-06


def dot(a, b):
    return jnp.dot(a, b, preferred_element_type=F32)


def attention_kernel(
    n_heads, hd, n_slots, lookup_ref, counts_ref, q_ref, do_ref, low_ref, own_ref, high_ref,
    att_ref, dq_ref, g_low_ref, g_own_ref, g_high_ref,
    kv_t, k_n, v_n, dk_acc, dv_acc, e_s, ds_s,
):
    cols = n_heads * hd
    wide = n_heads * BLK
    pieces = ((low_ref, g_low_ref), (own_ref, g_own_ref), (high_ref, g_high_ref))

    first = 0
    for ref, _ in pieces:
        blocks = ref.shape[1] // BLK

        @pl.loop(0, blocks)
        def _(i, ref=ref, first=first):
            at = pl.ds(pl.multiple_of(i * BLK, BLK), BLK)
            both = ref[:, at]
            kv_t[first + i] = both
            k_n[first + i] = both[:cols].T
            v_n[first + i] = both[cols:].T
            zero = jnp.zeros((BLK, cols), F32)
            dk_acc[first + i] = zero
            dv_acc[first + i] = zero

        first += blocks

    def diagonal(parts):
        rows = []
        for h in range(n_heads):
            zero = jnp.zeros((hd, BLK), BF16)
            rows.append(
                jnp.concatenate([parts[h] if g == h else zero for g in range(n_heads)], axis=1)
            )
        return jnp.concatenate(rows, axis=0)

    def of_head(value, h):
        return value[h * hd : (h + 1) * hd, h * BLK : (h + 1) * BLK]

    @pl.loop(0, q_ref.shape[1] // BLK)
    def _(b):
        at = pl.ds(pl.multiple_of(b * BLK, BLK), BLK)
        q_t = q_ref[:, at]
        do_t = do_ref[:, at]
        slots = [lookup_ref[b, j] for j in range(n_slots)]
        count = counts_ref[b]
        q_diag = diagonal([q_t[h * hd : (h + 1) * hd] for h in range(n_heads)])
        total = jnp.zeros((1, wide), F32)
        for j in range(n_slots):
            raised = jnp.exp2(dot(k_n[slots[j]], q_diag))
            raised = raised * jnp.where(j < count, 1.0, 0.0)
            total = total + jnp.sum(raised, axis=0, keepdims=True)
            e_s[j * BLK : (j + 1) * BLK, :] = raised.astype(BF16)
        values_t = jnp.concatenate([kv_t[s][cols:] for s in slots], axis=1)
        keys_t = jnp.concatenate([kv_t[s][:cols] for s in slots], axis=1)
        out = dot(values_t, e_s[...])
        share = 1.0 / total
        att, scaled, inner = [], [], []
        for h in range(n_heads):
            share_h = share[:, h * BLK : (h + 1) * BLK]
            att_h = of_head(out, h) * share_h
            do_h = do_t[h * hd : (h + 1) * hd].astype(F32) * share_h
            att.append(att_h)
            scaled.append(do_h.astype(BF16))
            inner.append(jnp.sum(att_h * do_h, axis=0, keepdims=True))
        att_ref[:, at] = jnp.concatenate(att, axis=0).astype(BF16)
        inner = jnp.concatenate(inner, axis=1)
        do_diag = diagonal(scaled)
        q_rows = q_diag.T
        do_rows = do_diag.T
        for j in range(n_slots):
            rows = slice(j * BLK, (j + 1) * BLK)
            e = e_s[rows, :]
            d = e.astype(F32) * (dot(v_n[slots[j]], do_diag) - inner)
            d = d.astype(BF16)
            ds_s[rows, :] = d
            dk_acc[slots[j]] += dot(d, q_rows)
            dv_acc[slots[j]] += dot(e, do_rows)
        dq = dot(keys_t, ds_s[...])
        dq = jnp.concatenate([of_head(dq, h) for h in range(n_heads)], axis=0)
        dq_ref[:, at] = (dq * SCORE_SCALE).astype(dq_ref.dtype)

    first = 0
    for ref, g_ref in pieces:
        blocks = ref.shape[1] // BLK

        @pl.loop(0, blocks)
        def _(i, g_ref=g_ref, first=first):
            at = pl.ds(pl.multiple_of(i * BLK, BLK), BLK)
            g_ref[:cols, at] = (dk_acc[first + i] * math.log(2.0)).T.astype(g_ref.dtype)
            g_ref[cols:, at] = dv_acc[first + i].T.astype(g_ref.dtype)

        first += blocks


def attention(lookup, counts, q_t, do_t, low, own, high, hd=32):
    cols, rows = q_t.shape
    n_heads = cols // hd
    n_slots = lookup.shape[1]
    ext = (low.shape[1] + own.shape[1] + high.shape[1]) // BLK
    smem = pl.BlockSpec(memory_space=pltpu.SMEM)
    vmem = pl.BlockSpec(memory_space=pltpu.VMEM)
    shape = jax.ShapeDtypeStruct
    return pl.pallas_call(
        functools.partial(attention_kernel, n_heads, hd, n_slots),
        out_shape=(
            shape((cols, rows), BF16),
            shape((cols, rows), BF16),
            shape(low.shape, BF16),
            shape(own.shape, F32),
            shape(high.shape, BF16),
        ),
        in_specs=[smem, smem] + [vmem] * 5,
        out_specs=(vmem,) * 5,
        scratch_shapes=[
            pltpu.VMEM((ext, 2 * cols, BLK), BF16),
            pltpu.VMEM((ext, BLK, cols), BF16),
            pltpu.VMEM((ext, BLK, cols), BF16),
            pltpu.VMEM((ext, BLK, cols), F32),
            pltpu.VMEM((ext, BLK, cols), F32),
            pltpu.VMEM((n_slots * BLK, n_heads * BLK), BF16),
            pltpu.VMEM((n_slots * BLK, n_heads * BLK), BF16),
        ],
        compiler_params=pltpu.CompilerParams(vmem_limit_bytes=52 * 1024 * 1024),
    )(lookup, counts, q_t, do_t, low, own, high)


def sums_kernel(
    n_slab, n_head, qkv_ref, out_part_ref, w_ref, gain_ref,
    d_qkv_ref, d_out_ref, d_gain_ref,
    heads_in, full, slabs_in, chunk, done_out, gain_part, gains_in,
    send_a, recv_a, send_b, recv_b, send_c, recv_c, send_d, recv_d, send_e, recv_e,
):
    slab, head = lax.axis_index("slab"), lax.axis_index("head")
    rows_q = qkv_ref.shape[0]
    rows_o = out_part_ref.shape[0] // n_head
    step = chunk.shape[0]

    def other_heads():
        return [(k, lax.rem(head + k, n_head)) for k in range(1, n_head)]

    def other_slabs():
        return [(k, lax.rem(slab + k, n_slab)) for k in range(1, n_slab)]

    barrier = pltpu.get_barrier_semaphore()
    for _, h in other_heads():
        pl.semaphore_signal(barrier, inc=1, device_id=(slab, h), device_id_type=MESH)
    for _, s in other_slabs():
        pl.semaphore_signal(barrier, inc=1, device_id=(s, head), device_id_type=MESH)
    pl.semaphore_wait(barrier, n_head + n_slab - 2)

    def send(src, dst, send_sem, recv_sem, target):
        copy = pltpu.make_async_remote_copy(
            src_ref=src, dst_ref=dst, send_sem=send_sem, recv_sem=recv_sem,
            device_id=target, device_id_type=MESH,
        )
        copy.start()
        return copy

    pending = []
    for k, h in other_heads():
        rows = pl.ds(pl.multiple_of(h * rows_o, 16), rows_o)
        pending.append(
            send(out_part_ref.at[rows], heads_in.at[k], send_a.at[k], recv_a.at[k], (slab, h))
        )
    full[:rows_q, :] = qkv_ref[...]
    if full.shape[0] > rows_q + rows_o:
        full[rows_q + rows_o :, :] = jnp.zeros(
            (full.shape[0] - rows_q - rows_o, full.shape[1]), BF16
        )
    mine = pl.ds(pl.multiple_of(head * rows_o, 16), rows_o)
    total = out_part_ref[mine, :].astype(F32)
    for k in range(1, n_head):
        pending[k - 1].wait()
        total += heads_in[k].astype(F32)
    full[rows_q : rows_q + rows_o, :] = total.astype(BF16)

    pending = []
    for k, s in other_slabs():
        rows = pl.ds(pl.multiple_of(s * step, 16), step)
        pending.append(send(full.at[rows], slabs_in.at[k], send_b.at[k], recv_b.at[k], (s, head)))
    mine = pl.ds(pl.multiple_of(slab * step, 16), step)
    total = full[mine, :].astype(F32)
    for k in range(1, n_slab):
        pending[k - 1].wait()
        total += slabs_in[k].astype(F32)
    chunk[...] = total.astype(BF16)
    pending = []
    for k, s in other_slabs():
        pending.append(send(chunk, done_out.at[mine], send_c.at[k], recv_c.at[k], (s, head)))
    done_out[mine, :] = chunk[...]
    for copy in pending:
        copy.wait()

    mine = pl.ds(pl.multiple_of(head * rows_o, 16), rows_o)
    own = done_out.at[pl.ds(rows_q, rows_o)]
    pending = []
    for k, h in other_heads():
        pending.append(send(own, heads_in.at[n_head + k], send_d.at[k], recv_d.at[k], (slab, h)))
    summed = done_out[:rows_q, :].astype(F32)
    part = jnp.sum(summed * w_ref[...].astype(F32), axis=0, keepdims=True) / gain_ref[...]
    gain_part[...] = jnp.broadcast_to(part, gain_part.shape)
    for k, h in other_heads():
        pending.append(send(gain_part, gains_in.at[k], send_e.at[k], recv_e.at[k], (slab, h)))
    d_qkv_ref[...] = summed
    d_out_ref[mine, :] = done_out[rows_q : rows_q + rows_o, :].astype(F32)
    for copy in pending:
        copy.wait()
    total = gain_part[...]
    for k in range(1, n_head):
        source = lax.rem(head + n_head - k, n_head)
        rows = pl.ds(pl.multiple_of(source * rows_o, 16), rows_o)
        d_out_ref[rows, :] = heads_in[n_head + k].astype(F32)
        total += gains_in[k]
    d_gain_ref[...] = total


def grad_sums(qkv_part, out_part, w_t, gain):
    n_slab, n_head = lax.axis_size("slab"), lax.axis_size("head")
    rows_q, width = qkv_part.shape
    rows_o = out_part.shape[0] // n_head
    step = -(-(rows_q + rows_o) // (16 * n_slab)) * 16
    vmem = pl.BlockSpec(memory_space=pltpu.VMEM)
    shape = jax.ShapeDtypeStruct
    dma = pltpu.SemaphoreType.DMA
    return pl.pallas_call(
        functools.partial(sums_kernel, n_slab, n_head),
        out_shape=(
            shape((rows_q, width), F32),
            shape(out_part.shape, F32),
            shape((8, width), F32),
        ),
        in_specs=[vmem] * 4,
        out_specs=(vmem,) * 3,
        scratch_shapes=[
            pltpu.VMEM((2 * n_head, rows_o, width), BF16),
            pltpu.VMEM((n_slab * step, width), BF16),
            pltpu.VMEM((n_slab, step, width), BF16),
            pltpu.VMEM((step, width), BF16),
            pltpu.VMEM((n_slab * step, width), BF16),
            pltpu.VMEM((8, width), F32),
            pltpu.VMEM((n_head, 8, width), F32),
        ]
        + [dma((n,)) for n in (n_head, n_head, n_slab, n_slab, n_slab, n_slab)]
        + [dma((n_head,))] * 4,
        compiler_params=pltpu.CompilerParams(
            collective_id=0, has_side_effects=True, vmem_limit_bytes=32 * 1024 * 1024
        ),
        cost_estimate=pl.CostEstimate(flops=0, bytes_accessed=30_000_000, transcendentals=0),
    )(qkv_part, out_part, w_t, gain)


def shifted(value, steps):
    size = lax.axis_size("slab")
    return lax.ppermute(value, "slab", [(i, (i + steps) % size) for i in range(size)])


def local(tokens, norm_gain, w_qkv, w_out, cotangent, neighbours, counts):
    width = tokens.shape[1]
    hd = width // HEADS
    n_head, n_slab = lax.axis_size("head"), lax.axis_size("slab")
    cols = width // n_head
    here = HEADS // n_head
    head_index, slab_index = lax.axis_index("head"), lax.axis_index("slab")
    slab_blocks, n_slots = neighbours.shape
    slab_rows = slab_blocks * BLK
    halo = REACH * BLK
    tok = tokens.astype(F32)
    inverse = lax.rsqrt(jnp.mean(tok * tok, -1, keepdims=True) + norm_eps)
    normed = (tok * inverse * norm_gain).astype(BF16)
    gathered = lax.all_gather(normed, "head", axis=0, tiled=True)
    w_here = lax.dynamic_slice_in_dim(w_qkv, head_index * cols, cols, 2)
    w_t = w_here.transpose(0, 2, 1).reshape(3 * cols, width)

    d_attended = lax.dot_general(
        w_out, cotangent, (((1,), (1,)), ((), ())), preferred_element_type=F32
    ).astype(BF16)
    d_heads = lax.all_to_all(d_attended, "head", split_axis=0, concat_axis=1, tiled=True)

    projected = lax.dot_general(
        w_t, gathered, (((1,), (1,)), ((), ())), preferred_element_type=F32
    )
    by_head = projected[: 2 * cols].reshape(2, here, hd, slab_rows)
    length = jnp.sqrt(jnp.sum(by_head * by_head, 2, keepdims=True))
    floor = 0.7 * math.sqrt(hd)
    divisor = jnp.maximum(length, floor)
    unit = by_head / divisor
    q_t = (unit[0] * (SCORE_SCALE * LOG2E)).reshape(cols, slab_rows).astype(BF16)
    kv_t = jnp.concatenate(
        [unit[1].reshape(cols, slab_rows).astype(BF16), projected[2 * cols :].astype(BF16)], 0
    )
    low = shifted(kv_t[:, slab_rows - halo :], 1)
    high = shifted(kv_t[:, :halo], -1)
    lookup = (neighbours - slab_index * slab_blocks + REACH) % (slab_blocks * n_slab)
    attended_t, dq_t, g_low, g_own, g_high = attention(
        lookup, counts, q_t, d_heads, low, kv_t, high, hd
    )
    from_above = shifted(g_low, -1).astype(F32)
    from_below = shifted(g_high, 1).astype(F32)

    attended = lax.all_to_all(attended_t, "head", split_axis=1, concat_axis=0, tiled=True)
    output = (
        tok
        + lax.dot_general(attended, w_out, (((0,), (0,)), ((), ())), preferred_element_type=F32)
    ).astype(BF16)
    d_out_part = dot(attended, cotangent)

    if slab_rows == halo:
        g_kv = g_own + from_above + from_below
    else:
        g_kv = g_own.at[:, slab_rows - halo :].add(from_above).at[:, :halo].add(from_below)
    along = jnp.stack([dq_t.astype(F32), g_kv[:cols]]).reshape(2, here, hd, slab_rows)
    inner = jnp.sum(unit * along, 2, keepdims=True)
    d_qk = (along - jnp.where(length > floor, unit * inner, 0.0)) / divisor
    d_qkv = jnp.concatenate(
        [d_qk.reshape(2 * cols, slab_rows).astype(BF16), g_kv[cols:].astype(BF16)], 0
    )
    d_normed = lax.psum_scatter(
        lax.dot_general(
            d_qkv, w_t, (((0,), (0,)), ((), ())), preferred_element_type=F32
        ).astype(BF16),
        "head",
        scatter_dimension=0,
        tiled=True,
    ).astype(F32)
    d_qkv_part = dot(d_qkv, gathered).astype(BF16)
    d_w, d_w_out, d_gain = grad_sums(
        d_qkv_part, d_out_part.astype(BF16), w_t, norm_gain.reshape(1, width)
    )
    d_w_qkv = d_w.reshape(3, cols, width).transpose(0, 2, 1)
    scaled = d_normed * norm_gain
    d_tokens = (
        cotangent.astype(F32)
        + inverse * scaled
        - tok * inverse**3 * jnp.mean(scaled * tok, -1, keepdims=True)
    )
    return (output, d_tokens.astype(BF16), d_w_qkv, d_w_out, d_gain[0])


def solution(mesh):
    placed = (
        P(("slab", "head"), None),
        P(),
        P(),
        P(),
        P(("slab", "head"), None),
        P("slab", None),
        P("slab"),
    )
    return jax.shard_map(
        local,
        mesh=mesh,
        in_specs=placed,
        out_specs=(
            P(("slab", "head"), None),
            P(("slab", "head"), None),
            P(None, None, "head"),
            P(),
            P(),
        ),
        check_vma=False,
    )
```

```python
import functools
import math

import jax
import jax.numpy as jnp
from jax import lax
from jax.experimental import pallas as pl
from jax.experimental.pallas import tpu as pltpu
from jax.sharding import PartitionSpec as P

HEADS = 12
BLK = 128
REACH = 16
MESH = pl.DeviceIdType.MESH
F32, BF16 = jnp.float32, jnp.bfloat16

SCORE_SCALE = 10.0
LOG2E = 1.0 / math.log(2.0)
norm_eps = 1e-06


def dot(a, b):
    return jnp.dot(a, b, preferred_element_type=F32)


def attention_kernel(
    n_heads, hd, n_slots, lookup_ref, counts_ref, q_ref, do_ref, kv_ref,
    att_ref, dq_ref, g_ref,
    kv_t, k_n, v_n, dk_acc, dv_acc, e_s, ds_s,
):
    cols = n_heads * hd
    wide = n_heads * BLK
    ext = kv_ref.shape[1] // BLK

    @pl.loop(0, ext)
    def _(i):
        both = kv_ref[:, pl.ds(pl.multiple_of(i * BLK, BLK), BLK)]
        kv_t[i] = both
        k_n[i] = both[:cols].T
        v_n[i] = both[cols:].T
        zero = jnp.zeros((BLK, cols), F32)
        dk_acc[i] = zero
        dv_acc[i] = zero

    def diagonal(parts):
        rows = []
        for h in range(n_heads):
            zero = jnp.zeros((hd, BLK), BF16)
            rows.append(
                jnp.concatenate([parts[h] if g == h else zero for g in range(n_heads)], axis=1)
            )
        return jnp.concatenate(rows, axis=0)

    def of_head(value, h):
        return value[h * hd : (h + 1) * hd, h * BLK : (h + 1) * BLK]

    @pl.loop(0, q_ref.shape[1] // BLK)
    def _(b):
        at = pl.ds(pl.multiple_of(b * BLK, BLK), BLK)
        q_t = q_ref[:, at]
        do_t = do_ref[:, at]
        slots = [lookup_ref[b, j] for j in range(n_slots)]
        count = counts_ref[b]
        q_diag = diagonal([q_t[h * hd : (h + 1) * hd] for h in range(n_heads)])
        total = jnp.zeros((1, wide), F32)
        for j in range(n_slots):
            raised = jnp.exp2(dot(k_n[slots[j]], q_diag))
            raised = raised * jnp.where(j < count, 1.0, 0.0)
            total = total + jnp.sum(raised, axis=0, keepdims=True)
            e_s[j * BLK : (j + 1) * BLK, :] = raised.astype(BF16)
        values_t = jnp.concatenate([kv_t[s][cols:] for s in slots], axis=1)
        keys_t = jnp.concatenate([kv_t[s][:cols] for s in slots], axis=1)
        out = dot(values_t, e_s[...])
        share = 1.0 / total
        att, scaled, inner = [], [], []
        for h in range(n_heads):
            share_h = share[:, h * BLK : (h + 1) * BLK]
            att_h = of_head(out, h) * share_h
            do_h = do_t[h * hd : (h + 1) * hd].astype(F32) * share_h
            att.append(att_h)
            scaled.append(do_h.astype(BF16))
            inner.append(jnp.sum(att_h * do_h, axis=0, keepdims=True))
        att_ref[:, at] = jnp.concatenate(att, axis=0).astype(BF16)
        inner = jnp.concatenate(inner, axis=1)
        do_diag = diagonal(scaled)
        q_rows = q_diag.T
        do_rows = do_diag.T
        for j in range(n_slots):
            rows = slice(j * BLK, (j + 1) * BLK)
            e = e_s[rows, :]
            d = e.astype(F32) * (dot(v_n[slots[j]], do_diag) - inner)
            d = d.astype(BF16)
            ds_s[rows, :] = d
            dk_acc[slots[j]] += dot(d, q_rows)
            dv_acc[slots[j]] += dot(e, do_rows)
        dq = dot(keys_t, ds_s[...])
        dq = jnp.concatenate([of_head(dq, h) for h in range(n_heads)], axis=0)
        dq_ref[:, at] = (dq * SCORE_SCALE).astype(dq_ref.dtype)

    @pl.loop(0, ext)
    def _(i):
        at = pl.ds(pl.multiple_of(i * BLK, BLK), BLK)
        g_ref[:cols, at] = (dk_acc[i] * math.log(2.0)).T.astype(g_ref.dtype)
        g_ref[cols:, at] = dv_acc[i].T.astype(g_ref.dtype)


def attention(lookup, counts, q_t, do_t, kv_ext, hd):
    cols, rows = q_t.shape
    n_heads = cols // hd
    n_slots = lookup.shape[1]
    ext = kv_ext.shape[1] // BLK
    smem = pl.BlockSpec(memory_space=pltpu.SMEM)
    vmem = pl.BlockSpec(memory_space=pltpu.VMEM)
    shape = jax.ShapeDtypeStruct
    return pl.pallas_call(
        functools.partial(attention_kernel, n_heads, hd, n_slots),
        out_shape=(
            shape((cols, rows), BF16),
            shape((cols, rows), BF16),
            shape(kv_ext.shape, BF16),
        ),
        in_specs=[smem, smem] + [vmem] * 3,
        out_specs=(vmem,) * 3,
        scratch_shapes=[
            pltpu.VMEM((ext, 2 * cols, BLK), BF16),
            pltpu.VMEM((ext, BLK, cols), BF16),
            pltpu.VMEM((ext, BLK, cols), BF16),
            pltpu.VMEM((ext, BLK, cols), F32),
            pltpu.VMEM((ext, BLK, cols), F32),
            pltpu.VMEM((n_slots * BLK, n_heads * BLK), BF16),
            pltpu.VMEM((n_slots * BLK, n_heads * BLK), BF16),
        ],
        compiler_params=pltpu.CompilerParams(vmem_limit_bytes=52 * 1024 * 1024),
    )(lookup, counts, q_t, do_t, kv_ext)


def sender(src, dst, send_sem, recv_sem, target):
    copy = pltpu.make_async_remote_copy(
        src_ref=src, dst_ref=dst, send_sem=send_sem, recv_sem=recv_sem,
        device_id=target, device_id_type=MESH,
    )
    copy.start()
    return copy


def gather_kernel(
    n_slab, n_head, normed_ref, d_att_ref, ext_ref, d_heads_ref,
    h_send, h_recv, x_send, x_recv, c_send, c_recv, f_send, f_recv, a_send, a_recv,
):
    slab, head = lax.axis_index("slab"), lax.axis_index("head")
    up, down = lax.rem(slab + 1, n_slab), lax.rem(slab + n_slab - 1, n_slab)
    core = (head // 2) * 2 + 1 - lax.rem(head, 2)
    across = lax.rem(head + 2, n_head)
    rows = normed_ref.shape[0]
    cols = d_heads_ref.shape[0]

    barrier = pltpu.get_barrier_semaphore()
    for s in (up, down):
        pl.semaphore_signal(barrier, inc=1, device_id=(s, head), device_id_type=MESH)
    for k in range(1, n_head):
        pl.semaphore_signal(
            barrier, inc=1, device_id=(slab, lax.rem(head + k, n_head)), device_id_type=MESH
        )
    pl.semaphore_wait(barrier, n_head + 1)

    def at(t, h):
        return ext_ref.at[t, h]

    def spread(t, src):
        return (
            sender(src, at(t, head), x_send.at[t], x_recv.at[t], (slab, across)),
            sender(src, at(t, head), c_send.at[t], c_recv.at[t], (slab, core)),
        )

    def forward(t):
        return sender(
            at(t, across), at(t, across), f_send.at[t], f_recv.at[t], (slab, core)
        )

    own = spread(1, normed_ref)
    to_up = sender(normed_ref, at(0, head), h_send.at[0], h_recv.at[0], (up, head))
    to_down = sender(normed_ref, at(2, head), h_send.at[1], h_recv.at[1], (down, head))
    mine = pl.ds(pl.multiple_of(head * rows, 128), rows)
    sent = []
    for k in range(1, n_head):
        h = lax.rem(head + k, n_head)
        sent.append(
            sender(
                d_att_ref.at[pl.ds(pl.multiple_of(h * cols, 16), cols)],
                d_heads_ref.at[:, mine],
                a_send.at[k], a_recv.at[k], (slab, h),
            )
        )
    d_heads_ref[:, mine] = d_att_ref[pl.ds(pl.multiple_of(head * cols, 16), cols), :]
    ext_ref[1, head] = normed_ref[...]

    own[0].wait_recv()
    own_f = forward(1)
    to_up.wait_recv()
    low = spread(0, at(0, head))
    to_down.wait_recv()
    high = spread(2, at(2, head))
    low[0].wait_recv()
    low_f = forward(0)
    high[0].wait_recv()
    high_f = forward(2)
    for copy in (to_up, to_down, own[0], low[0], high[0]):
        copy.wait_send()
    for copy in (own[1], low[1], high[1], own_f, low_f, high_f, *sent):
        copy.wait()


def gather_slabs(normed, d_attended):
    n_slab, n_head = lax.axis_size("slab"), lax.axis_size("head")
    rows, width = normed.shape
    cols = width // n_head
    vmem = pl.BlockSpec(memory_space=pltpu.VMEM)
    shape = jax.ShapeDtypeStruct
    dma = pltpu.SemaphoreType.DMA
    return pl.pallas_call(
        functools.partial(gather_kernel, n_slab, n_head),
        out_shape=(
            shape((3, n_head, rows, width), BF16),
            shape((cols, n_head * rows), BF16),
        ),
        in_specs=[vmem] * 2,
        out_specs=(vmem,) * 2,
        scratch_shapes=[dma((2,))] * 2 + [dma((3,))] * 6 + [dma((n_head,))] * 2,
        compiler_params=pltpu.CompilerParams(
            collective_id=1, has_side_effects=True, vmem_limit_bytes=32 * 1024 * 1024
        ),
    )(normed, d_attended)


def sums_kernel(
    n_slab, n_head, att_ref, cot_ref, low_ref, own_ref, high_ref, qkv_ref, w_ref, gain_ref,
    attended_ref, dn_ref, d_qkv_ref, d_out_ref, d_gain_ref,
    pair_in, pair_out, x_in, rim_out, rim_in,
    out_part, heads_in, full, slabs_in, chunk, done_out, gain_part, gains_in, outs_in,
    p_send, p_recv, x_send, x_recv, r_send, r_recv, t_send, t_recv,
    send_a, recv_a, send_b, recv_b, send_c, recv_c, send_d, recv_d, send_e, recv_e,
):
    slab, head = lax.axis_index("slab"), lax.axis_index("head")
    up, down = lax.rem(slab + 1, n_slab), lax.rem(slab + n_slab - 1, n_slab)
    core = (head // 2) * 2 + 1 - lax.rem(head, 2)
    across = lax.rem(head + 2, n_head)
    corner = lax.rem(core + 2, n_head)
    rows_q = qkv_ref.shape[0]
    rows_o = att_ref.shape[0]
    step = chunk.shape[0]
    rows = dn_ref.shape[0]
    parts = (low_ref, own_ref, high_ref)

    def other_heads():
        return [(k, lax.rem(head + k, n_head)) for k in range(1, n_head)]

    def other_slabs():
        return [(k, lax.rem(slab + k, n_slab)) for k in range(1, n_slab)]

    def of(h):
        return pl.ds(pl.multiple_of(h * rows, 128), rows)

    def out_rows(h):
        return pl.ds(pl.multiple_of(h * rows_o, 16), rows_o)

    barrier = pltpu.get_barrier_semaphore()
    for _, h in other_heads():
        pl.semaphore_signal(barrier, inc=1, device_id=(slab, h), device_id_type=MESH)
    for _, s in other_slabs():
        pl.semaphore_signal(barrier, inc=1, device_id=(s, head), device_id_type=MESH)
    pl.semaphore_wait(barrier, n_head + n_slab - 2)

    def send_pair(t):
        return [
            sender(
                parts[t].at[of(h)], pair_in.at[t, i], p_send.at[t, i], p_recv.at[t, i],
                (slab, core),
            )
            for i, h in enumerate((corner, core))
        ]

    def pair_sum(t, copies):
        copies[0].wait()
        pair_out[t] = (
            parts[t][of(across), :].astype(F32) + pair_in[t, 0].astype(F32)
        ).astype(BF16)
        return sender(pair_out.at[t], x_in.at[t], x_send.at[t], x_recv.at[t], (slab, across))

    def whole_sum(t):
        return (
            parts[t][of(head), :].astype(F32)
            + pair_in[t, 1].astype(F32)
            + x_in[t].astype(F32)
        )

    sent = []
    for k, h in other_heads():
        sent.append(
            sender(
                att_ref.at[:, of(h)], attended_ref.at[out_rows(head)],
                t_send.at[k], t_recv.at[k], (slab, h),
            )
        )
    pairs = {t: send_pair(t) for t in (0, 2, 1)}
    attended_ref[out_rows(head), :] = att_ref[:, of(head)]
    x_low = pair_sum(0, pairs[0])
    x_high = pair_sum(2, pairs[2])

    for copy in sent:
        copy.wait()
    out_part[...] = dot(attended_ref[...], cot_ref[...]).astype(BF16)
    sent = []
    for k, h in other_heads():
        sent.append(
            sender(
                out_part.at[out_rows(h)], heads_in.at[k], send_a.at[k], recv_a.at[k], (slab, h)
            )
        )
    full[:rows_q, :] = qkv_ref[...]
    if full.shape[0] > rows_q + rows_o:
        full[rows_q + rows_o :, :] = jnp.zeros(
            (full.shape[0] - rows_q - rows_o, full.shape[1]), BF16
        )
    x_own = pair_sum(1, pairs[1])
    total = out_part[out_rows(head), :].astype(F32)
    for k in range(1, n_head):
        sent[k - 1].wait()
        total += heads_in[k].astype(F32)
    full[rows_q : rows_q + rows_o, :] = total.astype(BF16)
    sent = []
    for k, s in other_slabs():
        part = pl.ds(pl.multiple_of(s * step, 16), step)
        sent.append(sender(full.at[part], slabs_in.at[k], send_b.at[k], recv_b.at[k], (s, head)))

    pairs[0][1].wait()
    x_low.wait()
    rim_out[0] = whole_sum(0).astype(BF16)
    to_down = sender(rim_out.at[0], rim_in.at[0], r_send.at[0], r_recv.at[0], (down, head))
    pairs[2][1].wait()
    x_high.wait()
    rim_out[1] = whole_sum(2).astype(BF16)
    to_up = sender(rim_out.at[1], rim_in.at[1], r_send.at[1], r_recv.at[1], (up, head))

    mine = pl.ds(pl.multiple_of(slab * step, 16), step)
    total = full[mine, :].astype(F32)
    for k in range(1, n_slab):
        sent[k - 1].wait()
        total += slabs_in[k].astype(F32)
    chunk[...] = total.astype(BF16)
    sent = []
    for k, s in other_slabs():
        sent.append(sender(chunk, done_out.at[mine], send_c.at[k], recv_c.at[k], (s, head)))
    done_out[mine, :] = chunk[...]
    pairs[1][1].wait()
    x_own.wait()
    dn_ref[...] = whole_sum(1)
    for copy in sent:
        copy.wait()

    own = done_out.at[pl.ds(rows_q, rows_o)]
    sent = []
    for k, h in other_heads():
        sent.append(sender(own, outs_in.at[k], send_d.at[k], recv_d.at[k], (slab, h)))
    summed = done_out[:rows_q, :].astype(F32)
    part = jnp.sum(summed * w_ref[...].astype(F32), axis=0, keepdims=True) / gain_ref[...]
    gain_part[...] = jnp.broadcast_to(part, gain_part.shape)
    for k, h in other_heads():
        sent.append(sender(gain_part, gains_in.at[k], send_e.at[k], recv_e.at[k], (slab, h)))
    d_qkv_ref[...] = summed
    d_out_ref[out_rows(head), :] = done_out[rows_q : rows_q + rows_o, :].astype(F32)
    to_down.wait()
    to_up.wait()
    dn_ref[...] += rim_in[0].astype(F32) + rim_in[1].astype(F32)
    for copy in sent:
        copy.wait()
    gains_in[0] = gain_part[...]
    total = jnp.zeros(gain_part.shape, F32)
    for h in range(n_head):
        total += gains_in[lax.rem(head + n_head - h, n_head)]
    for k in range(1, n_head):
        source = lax.rem(head + n_head - k, n_head)
        d_out_ref[out_rows(source), :] = outs_in[k].astype(F32)
    d_gain_ref[...] = total


def grad_sums(att_t, cotangent, low, own, high, qkv_part, w_t, gain):
    n_slab, n_head = lax.axis_size("slab"), lax.axis_size("head")
    rows_q, width = qkv_part.shape
    rows_o = att_t.shape[0]
    rows = cotangent.shape[0]
    step = -(-(rows_q + rows_o) // (16 * n_slab)) * 16
    vmem = pl.BlockSpec(memory_space=pltpu.VMEM)
    shape = jax.ShapeDtypeStruct
    dma = pltpu.SemaphoreType.DMA
    return pl.pallas_call(
        functools.partial(sums_kernel, n_slab, n_head),
        out_shape=(
            shape((width, rows), BF16),
            shape((rows, width), F32),
            shape((rows_q, width), F32),
            shape((width, width), F32),
            shape((8, width), F32),
        ),
        in_specs=[vmem] * 8,
        out_specs=(vmem,) * 5,
        scratch_shapes=[
            pltpu.VMEM((3, 2, rows, width), BF16),
            pltpu.VMEM((3, rows, width), BF16),
            pltpu.VMEM((3, rows, width), BF16),
            pltpu.VMEM((2, rows, width), BF16),
            pltpu.VMEM((2, rows, width), BF16),
            pltpu.VMEM((width, width), BF16),
            pltpu.VMEM((n_head, rows_o, width), BF16),
            pltpu.VMEM((n_slab * step, width), BF16),
            pltpu.VMEM((n_slab, step, width), BF16),
            pltpu.VMEM((step, width), BF16),
            pltpu.VMEM((n_slab * step, width), BF16),
            pltpu.VMEM((8, width), F32),
            pltpu.VMEM((n_head, 8, width), F32),
            pltpu.VMEM((n_head, rows_o, width), BF16),
        ]
        + [dma((3, 2))] * 2 + [dma((3,))] * 2 + [dma((2,))] * 2 + [dma((n_head,))] * 4
        + [dma((n_slab,))] * 4 + [dma((n_head,))] * 4,
        compiler_params=pltpu.CompilerParams(
            collective_id=0, has_side_effects=True, vmem_limit_bytes=48 * 1024 * 1024
        ),
    )(att_t, cotangent, low, own, high, qkv_part, w_t, gain)


def over_rows(a, b):
    return lax.dot_general(a, b, (((0,), (0,)), ((), ())), preferred_element_type=F32)


def over_width(a, b):
    return lax.dot_general(a, b, (((1,), (1,)), ((), ())), preferred_element_type=F32)


def local(tokens, norm_gain, w_qkv, w_out, cotangent, neighbours, counts):
    width = tokens.shape[1]
    hd = width // HEADS
    n_head, n_slab = lax.axis_size("head"), lax.axis_size("slab")
    cols = width // n_head
    here = HEADS // n_head
    head_index, slab_index = lax.axis_index("head"), lax.axis_index("slab")
    slab_blocks = neighbours.shape[0]
    slab_rows = slab_blocks * BLK
    tok = tokens.astype(F32)
    inverse = lax.rsqrt(jnp.mean(tok * tok, -1, keepdims=True) + norm_eps)
    normed = (tok * inverse * norm_gain).astype(BF16)
    w_here = lax.dynamic_slice_in_dim(w_qkv, head_index * cols, cols, 2)
    w_t = w_here.transpose(0, 2, 1).reshape(3 * cols, width)
    d_attended = over_width(w_out, cotangent).astype(BF16)
    gathered, d_heads = gather_slabs(normed, d_attended)
    gathered = gathered.reshape(3 * slab_rows, width)
    own_rows = gathered[slab_rows : 2 * slab_rows]

    floor = 0.7 * math.sqrt(hd)

    def unit_of(projected):
        by_head = projected.reshape(here, hd, -1)
        length = jnp.sqrt(jnp.sum(by_head * by_head, 1, keepdims=True))
        divisor = jnp.maximum(length, floor)
        return by_head / divisor, divisor, length > floor

    def unit_back(parts, grad):
        unit, divisor, active = parts
        along = grad.astype(F32).reshape(unit.shape)
        inner = jnp.sum(unit * along, 1, keepdims=True)
        result = (along - jnp.where(active, unit * inner, 0.0)) / divisor
        return result.reshape(grad.shape).astype(BF16)

    q_parts = unit_of(over_width(w_t[:cols], own_rows))
    kv = over_width(w_t[cols:], gathered)
    k_parts = unit_of(kv[:cols])
    q_t = (q_parts[0] * (SCORE_SCALE * LOG2E)).reshape(cols, slab_rows).astype(BF16)
    kv_ext = jnp.concatenate(
        [k_parts[0].reshape(cols, 3 * slab_rows).astype(BF16), kv[cols:].astype(BF16)], 0
    )
    lookup = (neighbours - slab_index * slab_blocks + REACH) % (slab_blocks * n_slab)
    att_t, dq_t, g_kv = attention(lookup, counts, q_t, d_heads, kv_ext, hd)

    d_q = unit_back(q_parts, dq_t)
    d_kv = jnp.concatenate([unit_back(k_parts, g_kv[:cols]), g_kv[cols:]], 0)
    low, high = d_kv[:, :slab_rows], d_kv[:, 2 * slab_rows :]
    own = jnp.concatenate([d_q, d_kv[:, slab_rows : 2 * slab_rows]], 0)
    qkv_part = jnp.concatenate([dot(d_q, own_rows), dot(d_kv, gathered)], 0).astype(BF16)
    attended, d_normed, d_w, d_w_out, d_gain = grad_sums(
        att_t,
        cotangent,
        over_rows(low, w_t[cols:]).astype(BF16),
        over_rows(own, w_t).astype(BF16),
        over_rows(high, w_t[cols:]).astype(BF16),
        qkv_part,
        w_t,
        norm_gain.reshape(1, width),
    )
    output = (tok + over_rows(attended, w_out)).astype(BF16)
    d_w_qkv = d_w.reshape(3, cols, width).transpose(0, 2, 1)
    scaled = d_normed * norm_gain
    d_tokens = (
        cotangent.astype(F32)
        + inverse * scaled
        - tok * inverse**3 * jnp.mean(scaled * tok, -1, keepdims=True)
    )
    return (output, d_tokens.astype(BF16), d_w_qkv, d_w_out, d_gain[0])


def solution(mesh):
    placed = (
        P(("slab", "head"), None),
        P(),
        P(),
        P(),
        P(("slab", "head"), None),
        P("slab", None),
        P("slab"),
    )
    return jax.shard_map(
        local,
        mesh=mesh,
        in_specs=placed,
        out_specs=(
            P(("slab", "head"), None),
            P(("slab", "head"), None),
            P(None, None, "head"),
            P(),
            P(),
        ),
        check_vma=False,
    )
```

```python
import functools
import math

import jax
import jax.numpy as jnp
from jax import lax
from jax.experimental import pallas as pl
from jax.experimental.pallas import tpu as pltpu
from jax.sharding import PartitionSpec as P

HEADS = 12
BLK = 128
REACH = 16
MESH = pl.DeviceIdType.MESH
F32, BF16 = jnp.float32, jnp.bfloat16

SCORE_SCALE = 10.0
LOG2E = 1.0 / math.log(2.0)
norm_eps = 1e-06


def dot(a, b):
    return jnp.dot(a, b, preferred_element_type=F32)


def attention_kernel(
    n_heads, hd, n_slots, lookup_ref, counts_ref, q_ref, do_ref, kv_ref,
    att_ref, dq_ref, g_ref,
    kv_t, k_n, v_n, dk_acc, dv_acc, e_s, ds_s,
):
    cols = n_heads * hd
    wide = n_heads * BLK
    ext = kv_ref.shape[1] // BLK

    @pl.loop(0, ext)
    def _(i):
        both = kv_ref[:, pl.ds(pl.multiple_of(i * BLK, BLK), BLK)]
        kv_t[i] = both
        k_n[i] = both[:cols].T
        v_n[i] = both[cols:].T
        zero = jnp.zeros((BLK, cols), F32)
        dk_acc[i] = zero
        dv_acc[i] = zero

    def diagonal(parts):
        rows = []
        for h in range(n_heads):
            zero = jnp.zeros((hd, BLK), BF16)
            rows.append(
                jnp.concatenate([parts[h] if g == h else zero for g in range(n_heads)], axis=1)
            )
        return jnp.concatenate(rows, axis=0)

    def of_head(value, h):
        return value[h * hd : (h + 1) * hd, h * BLK : (h + 1) * BLK]

    @pl.loop(0, q_ref.shape[1] // BLK)
    def _(b):
        at = pl.ds(pl.multiple_of(b * BLK, BLK), BLK)
        q_t = q_ref[:, at]
        do_t = do_ref[:, at]
        slots = [lookup_ref[b, j] for j in range(n_slots)]
        count = counts_ref[b]
        q_diag = diagonal([q_t[h * hd : (h + 1) * hd] for h in range(n_heads)])
        total = jnp.zeros((1, wide), F32)
        for j in range(n_slots):
            raised = jnp.exp2(dot(k_n[slots[j]], q_diag))
            raised = raised * jnp.where(j < count, 1.0, 0.0)
            total = total + jnp.sum(raised, axis=0, keepdims=True)
            e_s[j * BLK : (j + 1) * BLK, :] = raised.astype(BF16)
        values_t = jnp.concatenate([kv_t[s][cols:] for s in slots], axis=1)
        keys_t = jnp.concatenate([kv_t[s][:cols] for s in slots], axis=1)
        out = dot(values_t, e_s[...])
        share = 1.0 / total
        att, scaled, inner = [], [], []
        for h in range(n_heads):
            share_h = share[:, h * BLK : (h + 1) * BLK]
            att_h = of_head(out, h) * share_h
            do_h = do_t[h * hd : (h + 1) * hd].astype(F32) * share_h
            att.append(att_h)
            scaled.append(do_h.astype(BF16))
            inner.append(jnp.sum(att_h * do_h, axis=0, keepdims=True))
        att_ref[:, at] = jnp.concatenate(att, axis=0).astype(BF16)
        inner = jnp.concatenate(inner, axis=1)
        do_diag = diagonal(scaled)
        q_rows = q_diag.T
        do_rows = do_diag.T
        for j in range(n_slots):
            rows = slice(j * BLK, (j + 1) * BLK)
            e = e_s[rows, :]
            d = e.astype(F32) * (dot(v_n[slots[j]], do_diag) - inner)
            d = d.astype(BF16)
            ds_s[rows, :] = d
            dk_acc[slots[j]] += dot(d, q_rows)
            dv_acc[slots[j]] += dot(e, do_rows)
        dq = dot(keys_t, ds_s[...])
        dq = jnp.concatenate([of_head(dq, h) for h in range(n_heads)], axis=0)
        dq_ref[:, at] = (dq * SCORE_SCALE).astype(dq_ref.dtype)

    @pl.loop(0, ext)
    def _(i):
        at = pl.ds(pl.multiple_of(i * BLK, BLK), BLK)
        g_ref[:cols, at] = (dk_acc[i] * math.log(2.0)).T.astype(g_ref.dtype)
        g_ref[cols:, at] = dv_acc[i].T.astype(g_ref.dtype)


def attention(lookup, counts, q_t, do_t, kv_ext, hd):
    cols, rows = q_t.shape
    n_heads = cols // hd
    n_slots = lookup.shape[1]
    ext = kv_ext.shape[1] // BLK
    smem = pl.BlockSpec(memory_space=pltpu.SMEM)
    vmem = pl.BlockSpec(memory_space=pltpu.VMEM)
    shape = jax.ShapeDtypeStruct
    return pl.pallas_call(
        functools.partial(attention_kernel, n_heads, hd, n_slots),
        out_shape=(
            shape((cols, rows), BF16),
            shape((cols, rows), BF16),
            shape(kv_ext.shape, BF16),
        ),
        in_specs=[smem, smem] + [vmem] * 3,
        out_specs=(vmem,) * 3,
        scratch_shapes=[
            pltpu.VMEM((ext, 2 * cols, BLK), BF16),
            pltpu.VMEM((ext, BLK, cols), BF16),
            pltpu.VMEM((ext, BLK, cols), BF16),
            pltpu.VMEM((ext, BLK, cols), F32),
            pltpu.VMEM((ext, BLK, cols), F32),
            pltpu.VMEM((n_slots * BLK, n_heads * BLK), BF16),
            pltpu.VMEM((n_slots * BLK, n_heads * BLK), BF16),
        ],
        compiler_params=pltpu.CompilerParams(vmem_limit_bytes=52 * 1024 * 1024),
    )(lookup, counts, q_t, do_t, kv_ext)


def sender(src, dst, send_sem, recv_sem, target):
    copy = pltpu.make_async_remote_copy(
        src_ref=src, dst_ref=dst, send_sem=send_sem, recv_sem=recv_sem,
        device_id=target, device_id_type=MESH,
    )
    copy.start()
    return copy


def gather_kernel(
    n_slab, n_head, normed_ref, d_att_ref, ext_ref, d_heads_ref,
    h_send, h_recv, x_send, x_recv, c_send, c_recv, f_send, f_recv, a_send, a_recv,
):
    slab, head = lax.axis_index("slab"), lax.axis_index("head")
    up, down = lax.rem(slab + 1, n_slab), lax.rem(slab + n_slab - 1, n_slab)
    core = (head // 2) * 2 + 1 - lax.rem(head, 2)
    across = lax.rem(head + 2, n_head)
    rows = normed_ref.shape[0]
    cols = d_heads_ref.shape[0]

    barrier = pltpu.get_barrier_semaphore()
    for s in (up, down):
        pl.semaphore_signal(barrier, inc=1, device_id=(s, head), device_id_type=MESH)
    for k in range(1, n_head):
        pl.semaphore_signal(
            barrier, inc=1, device_id=(slab, lax.rem(head + k, n_head)), device_id_type=MESH
        )
    pl.semaphore_wait(barrier, n_head + 1)

    n_chunks = h_send.shape[1]
    size = rows // n_chunks

    def at(t, h, c):
        return ext_ref.at[t, h, pl.ds(c * size, size)]

    def spread(t, c, src):
        return [
            sender(src, at(t, head, c), x_send.at[t, c], x_recv.at[t, c], (slab, across)),
            sender(src, at(t, head, c), c_send.at[t, c], c_recv.at[t, c], (slab, core)),
        ]

    def forward(t, c):
        return sender(
            at(t, across, c), at(t, across, c), f_send.at[t, c], f_recv.at[t, c], (slab, core)
        )

    own, low, high, to_up, to_down, ahead = [], [], [], [], [], []
    for c in range(n_chunks):
        src = normed_ref.at[pl.ds(c * size, size)]
        to_up.append(sender(src, at(0, head, c), h_send.at[0, c], h_recv.at[0, c], (up, head)))
        to_down.append(
            sender(src, at(2, head, c), h_send.at[1, c], h_recv.at[1, c], (down, head))
        )
        own.append(spread(1, c, src))
    mine = pl.ds(pl.multiple_of(head * rows, 128), rows)
    d_heads_ref[:, mine] = d_att_ref[pl.ds(pl.multiple_of(head * cols, 16), cols), :]
    ext_ref[1, head] = normed_ref[...]
    for c in range(n_chunks):
        to_up[c].wait_recv()
        low.append(spread(0, c, at(0, head, c)))
        to_down[c].wait_recv()
        high.append(spread(2, c, at(2, head, c)))
        own[c][0].wait_recv()
        ahead.append(forward(1, c))
    sent = []
    for k in range(1, n_head):
        h = lax.rem(head + k, n_head)
        sent.append(
            sender(
                d_att_ref.at[pl.ds(pl.multiple_of(h * cols, 16), cols)],
                d_heads_ref.at[:, mine],
                a_send.at[k], a_recv.at[k], (slab, h),
            )
        )
    for c in range(n_chunks):
        low[c][0].wait_recv()
        ahead.append(forward(0, c))
        high[c][0].wait_recv()
        ahead.append(forward(2, c))
    for c in range(n_chunks):
        for copy in (to_up[c], to_down[c], own[c][0], low[c][0], high[c][0]):
            copy.wait_send()
        for copy in (own[c][1], low[c][1], high[c][1]):
            copy.wait()
    for copy in (*ahead, *sent):
        copy.wait()


def gather_slabs(normed, d_attended):
    n_slab, n_head = lax.axis_size("slab"), lax.axis_size("head")
    rows, width = normed.shape
    cols = width // n_head
    vmem = pl.BlockSpec(memory_space=pltpu.VMEM)
    shape = jax.ShapeDtypeStruct
    dma = pltpu.SemaphoreType.DMA
    return pl.pallas_call(
        functools.partial(gather_kernel, n_slab, n_head),
        out_shape=(
            shape((3, n_head, rows, width), BF16),
            shape((cols, n_head * rows), BF16),
        ),
        in_specs=[vmem] * 2,
        out_specs=(vmem,) * 2,
        scratch_shapes=[dma((2, 4))] * 2 + [dma((3, 4))] * 6 + [dma((n_head,))] * 2,
        compiler_params=pltpu.CompilerParams(
            collective_id=1, has_side_effects=True, vmem_limit_bytes=32 * 1024 * 1024
        ),
    )(normed, d_attended)


def sums_kernel(
    n_slab, n_head, att_ref, cot_ref, low_ref, own_ref, high_ref, qkv_ref, w_ref, gain_ref,
    attended_ref, dn_ref, d_qkv_ref, d_out_ref, d_gain_ref,
    pair_in, pair_out, x_in, rim_out, rim_in,
    out_part, heads_in, full, slabs_in, chunk, done_out, gain_part, gains_in, outs_in,
    p_send, p_recv, x_send, x_recv, r_send, r_recv, t_send, t_recv,
    send_a, recv_a, send_b, recv_b, send_c, recv_c, send_d, recv_d, send_e, recv_e,
):
    slab, head = lax.axis_index("slab"), lax.axis_index("head")
    up, down = lax.rem(slab + 1, n_slab), lax.rem(slab + n_slab - 1, n_slab)
    core = (head // 2) * 2 + 1 - lax.rem(head, 2)
    across = lax.rem(head + 2, n_head)
    corner = lax.rem(core + 2, n_head)
    rows_q = qkv_ref.shape[0]
    rows_o = att_ref.shape[0]
    step = chunk.shape[0]
    rows = dn_ref.shape[0]
    parts = (low_ref, own_ref, high_ref)

    def other_heads():
        return [(k, lax.rem(head + k, n_head)) for k in range(1, n_head)]

    def other_slabs():
        return [(k, lax.rem(slab + k, n_slab)) for k in range(1, n_slab)]

    def of(h):
        return pl.ds(pl.multiple_of(h * rows, 128), rows)

    def out_rows(h):
        return pl.ds(pl.multiple_of(h * rows_o, 16), rows_o)

    barrier = pltpu.get_barrier_semaphore()
    for _, h in other_heads():
        pl.semaphore_signal(barrier, inc=1, device_id=(slab, h), device_id_type=MESH)
    for _, s in other_slabs():
        pl.semaphore_signal(barrier, inc=1, device_id=(s, head), device_id_type=MESH)
    pl.semaphore_wait(barrier, n_head + n_slab - 2)

    n_chunks = x_send.shape[1]
    size = rows // n_chunks

    def span(c):
        return pl.ds(c * size, size)

    def of_chunk(h, c):
        return pl.ds(pl.multiple_of(h * rows + c * size, 128), size)

    def send_pair(t, c, i):
        return sender(
            parts[t].at[of_chunk((corner, core)[i], c)], pair_in.at[t, i, span(c)],
            p_send.at[t, i, c], p_recv.at[t, i, c], (slab, core),
        )

    def pair_sum(t, c, copy):
        copy.wait()
        pair_out[t, span(c)] = (
            parts[t][of_chunk(across, c), :].astype(F32) + pair_in[t, 0, span(c)].astype(F32)
        ).astype(BF16)
        return sender(
            pair_out.at[t, span(c)], x_in.at[t, span(c)],
            x_send.at[t, c], x_recv.at[t, c], (slab, across),
        )

    def whole_sum(t, c):
        return (
            parts[t][of_chunk(head, c), :].astype(F32)
            + pair_in[t, 1, span(c)].astype(F32)
            + x_in[t, span(c)].astype(F32)
        )

    def rim(i, t, c, target):
        pairs[t, c, 1].wait()
        crossing[t, c].wait()
        rim_out[i, span(c)] = whole_sum(t, c).astype(BF16)
        return sender(
            rim_out.at[i, span(c)], rim_in.at[i, span(c)],
            r_send.at[i, c], r_recv.at[i, c], (target, head),
        )

    sent = []
    for k, h in other_heads():
        sent.append(
            sender(
                att_ref.at[:, of(h)], attended_ref.at[out_rows(head)],
                t_send.at[k], t_recv.at[k], (slab, h),
            )
        )
    pairs, crossing, rims = {}, {}, []
    order = [(t, c) for c in range(n_chunks) for t in (0, 2)]
    order += [(1, c) for c in range(n_chunks)]
    for i in range(2):
        for t, c in order:
            pairs[t, c, i] = send_pair(t, c, i)
    attended_ref[out_rows(head), :] = att_ref[:, of(head)]
    full[:rows_q, :] = qkv_ref[...]
    if full.shape[0] > rows_q + rows_o:
        full[rows_q + rows_o :, :] = jnp.zeros(
            (full.shape[0] - rows_q - rows_o, full.shape[1]), BF16
        )
    half = len(order) // 3
    for t, c in order[:half]:
        crossing[t, c] = pair_sum(t, c, pairs[t, c, 0])

    for copy in sent:
        copy.wait()
    out_part[...] = dot(attended_ref[...], cot_ref[...]).astype(BF16)
    sent = []
    for k, h in other_heads():
        sent.append(
            sender(
                out_part.at[out_rows(h)], heads_in.at[k], send_a.at[k], recv_a.at[k], (slab, h)
            )
        )
    for t, c in order[half:]:
        crossing[t, c] = pair_sum(t, c, pairs[t, c, 0])
    for t, c in order[:half]:
        rims.append(rim(t // 2, t, c, (down, None, up)[t]))

    total = out_part[out_rows(head), :].astype(F32)
    for k in range(1, n_head):
        sent[k - 1].wait()
        total += heads_in[k].astype(F32)
    full[rows_q : rows_q + rows_o, :] = total.astype(BF16)
    sent = []
    for k, s in other_slabs():
        part = pl.ds(pl.multiple_of(s * step, 16), step)
        sent.append(sender(full.at[part], slabs_in.at[k], send_b.at[k], recv_b.at[k], (s, head)))
    for t, c in order[half : 2 * half]:
        rims.append(rim(t // 2, t, c, (down, None, up)[t]))

    mine = pl.ds(pl.multiple_of(slab * step, 16), step)
    total = full[mine, :].astype(F32)
    for k in range(1, n_slab):
        sent[k - 1].wait()
        total += slabs_in[k].astype(F32)
    chunk[...] = total.astype(BF16)
    sent = []
    for k, s in other_slabs():
        sent.append(sender(chunk, done_out.at[mine], send_c.at[k], recv_c.at[k], (s, head)))
    done_out[mine, :] = chunk[...]
    for t, c in order[2 * half :]:
        pairs[t, c, 1].wait()
        crossing[t, c].wait()
        dn_ref[span(c), :] = whole_sum(t, c)
    for copy in sent:
        copy.wait()

    own = done_out.at[pl.ds(rows_q, rows_o)]
    sent = []
    for k, h in other_heads():
        sent.append(sender(own, outs_in.at[k], send_d.at[k], recv_d.at[k], (slab, h)))
    summed = done_out[:rows_q, :].astype(F32)
    part = jnp.sum(summed * w_ref[...].astype(F32), axis=0, keepdims=True) / gain_ref[...]
    gain_part[...] = jnp.broadcast_to(part, gain_part.shape)
    for k, h in other_heads():
        sent.append(sender(gain_part, gains_in.at[k], send_e.at[k], recv_e.at[k], (slab, h)))
    d_qkv_ref[...] = summed
    d_out_ref[out_rows(head), :] = done_out[rows_q : rows_q + rows_o, :].astype(F32)
    for copy in rims:
        copy.wait()
    dn_ref[...] += rim_in[0].astype(F32) + rim_in[1].astype(F32)
    for copy in sent:
        copy.wait()
    gains_in[0] = gain_part[...]
    total = jnp.zeros(gain_part.shape, F32)
    for h in range(n_head):
        total += gains_in[lax.rem(head + n_head - h, n_head)]
    for k in range(1, n_head):
        source = lax.rem(head + n_head - k, n_head)
        d_out_ref[out_rows(source), :] = outs_in[k].astype(F32)
    d_gain_ref[...] = total


def grad_sums(att_t, cotangent, low, own, high, qkv_part, w_t, gain):
    n_slab, n_head = lax.axis_size("slab"), lax.axis_size("head")
    rows_q, width = qkv_part.shape
    rows_o = att_t.shape[0]
    rows = cotangent.shape[0]
    step = -(-(rows_q + rows_o) // (16 * n_slab)) * 16
    vmem = pl.BlockSpec(memory_space=pltpu.VMEM)
    shape = jax.ShapeDtypeStruct
    dma = pltpu.SemaphoreType.DMA
    return pl.pallas_call(
        functools.partial(sums_kernel, n_slab, n_head),
        out_shape=(
            shape((width, rows), BF16),
            shape((rows, width), F32),
            shape((rows_q, width), F32),
            shape((width, width), F32),
            shape((8, width), F32),
        ),
        in_specs=[vmem] * 8,
        out_specs=(vmem,) * 5,
        scratch_shapes=[
            pltpu.VMEM((3, 2, rows, width), BF16),
            pltpu.VMEM((3, rows, width), BF16),
            pltpu.VMEM((3, rows, width), BF16),
            pltpu.VMEM((2, rows, width), BF16),
            pltpu.VMEM((2, rows, width), BF16),
            pltpu.VMEM((width, width), BF16),
            pltpu.VMEM((n_head, rows_o, width), BF16),
            pltpu.VMEM((n_slab * step, width), BF16),
            pltpu.VMEM((n_slab, step, width), BF16),
            pltpu.VMEM((step, width), BF16),
            pltpu.VMEM((n_slab * step, width), BF16),
            pltpu.VMEM((8, width), F32),
            pltpu.VMEM((n_head, 8, width), F32),
            pltpu.VMEM((n_head, rows_o, width), BF16),
        ]
        + [dma((3, 2, 4))] * 2 + [dma((3, 4))] * 2 + [dma((2, 4))] * 2 + [dma((n_head,))] * 4
        + [dma((n_slab,))] * 4 + [dma((n_head,))] * 4,
        compiler_params=pltpu.CompilerParams(
            collective_id=0, has_side_effects=True, vmem_limit_bytes=48 * 1024 * 1024
        ),
    )(att_t, cotangent, low, own, high, qkv_part, w_t, gain)


def over_rows(a, b):
    return lax.dot_general(a, b, (((0,), (0,)), ((), ())), preferred_element_type=F32)


def over_width(a, b):
    return lax.dot_general(a, b, (((1,), (1,)), ((), ())), preferred_element_type=F32)


def local(tokens, norm_gain, w_qkv, w_out, cotangent, neighbours, counts):
    width = tokens.shape[1]
    hd = width // HEADS
    n_head, n_slab = lax.axis_size("head"), lax.axis_size("slab")
    cols = width // n_head
    here = HEADS // n_head
    head_index, slab_index = lax.axis_index("head"), lax.axis_index("slab")
    slab_blocks = neighbours.shape[0]
    slab_rows = slab_blocks * BLK
    tok = tokens.astype(F32)
    inverse = lax.rsqrt(jnp.mean(tok * tok, -1, keepdims=True) + norm_eps)
    normed = (tok * inverse * norm_gain).astype(BF16)
    w_here = lax.dynamic_slice_in_dim(w_qkv, head_index * cols, cols, 2)
    w_t = w_here.transpose(0, 2, 1).reshape(3 * cols, width)
    d_attended = over_width(w_out, cotangent).astype(BF16)
    gathered, d_heads = gather_slabs(normed, d_attended)
    gathered = gathered.reshape(3 * slab_rows, width)
    own_rows = gathered[slab_rows : 2 * slab_rows]

    floor = 0.7 * math.sqrt(hd)

    def unit_of(projected):
        by_head = projected.reshape(here, hd, -1)
        length = jnp.sqrt(jnp.sum(by_head * by_head, 1, keepdims=True))
        divisor = jnp.maximum(length, floor)
        return by_head / divisor, divisor, length > floor

    def unit_back(parts, grad):
        unit, divisor, active = parts
        along = grad.astype(F32).reshape(unit.shape)
        inner = jnp.sum(unit * along, 1, keepdims=True)
        result = (along - jnp.where(active, unit * inner, 0.0)) / divisor
        return result.reshape(grad.shape).astype(BF16)

    q_parts = unit_of(over_width(w_t[:cols], own_rows))
    kv = over_width(w_t[cols:], gathered)
    k_parts = unit_of(kv[:cols])
    q_t = (q_parts[0] * (SCORE_SCALE * LOG2E)).reshape(cols, slab_rows).astype(BF16)
    kv_ext = jnp.concatenate(
        [k_parts[0].reshape(cols, 3 * slab_rows).astype(BF16), kv[cols:].astype(BF16)], 0
    )
    lookup = (neighbours - slab_index * slab_blocks + REACH) % (slab_blocks * n_slab)
    att_t, dq_t, g_kv = attention(lookup, counts, q_t, d_heads, kv_ext, hd)

    d_q = unit_back(q_parts, dq_t)
    d_kv = jnp.concatenate([unit_back(k_parts, g_kv[:cols]), g_kv[cols:]], 0)
    low, high = d_kv[:, :slab_rows], d_kv[:, 2 * slab_rows :]
    own = jnp.concatenate([d_q, d_kv[:, slab_rows : 2 * slab_rows]], 0)
    qkv_part = jnp.concatenate([dot(d_q, own_rows), dot(d_kv, gathered)], 0).astype(BF16)
    attended, d_normed, d_w, d_w_out, d_gain = grad_sums(
        att_t,
        cotangent,
        over_rows(low, w_t[cols:]).astype(BF16),
        over_rows(own, w_t).astype(BF16),
        over_rows(high, w_t[cols:]).astype(BF16),
        qkv_part,
        w_t,
        norm_gain.reshape(1, width),
    )
    output = (tok + over_rows(attended, w_out)).astype(BF16)
    d_w_qkv = d_w.reshape(3, cols, width).transpose(0, 2, 1)
    scaled = d_normed * norm_gain
    d_tokens = (
        cotangent.astype(F32)
        + inverse * scaled
        - tok * inverse**3 * jnp.mean(scaled * tok, -1, keepdims=True)
    )
    return (output, d_tokens.astype(BF16), d_w_qkv, d_w_out, d_gain[0])


def solution(mesh):
    placed = (
        P(("slab", "head"), None),
        P(),
        P(),
        P(),
        P(("slab", "head"), None),
        P("slab", None),
        P("slab"),
    )
    return jax.shard_map(
        local,
        mesh=mesh,
        in_specs=placed,
        out_specs=(
            P(("slab", "head"), None),
            P(("slab", "head"), None),
            P(None, None, "head"),
            P(),
            P(),
        ),
        check_vma=False,
    )
```

```python
import functools
import math

import jax
import jax.numpy as jnp
from jax import lax
from jax.experimental import pallas as pl
from jax.experimental.pallas import tpu as pltpu
from jax.sharding import PartitionSpec as P

HEADS = 12
BLK = 128
REACH = 16
MESH = pl.DeviceIdType.MESH
F32, BF16 = jnp.float32, jnp.bfloat16

SCORE_SCALE = 10.0
LOG2E = 1.0 / math.log(2.0)
norm_eps = 1e-06


def dot(a, b):
    return jnp.dot(a, b, preferred_element_type=F32)


def attention_kernel(
    n_heads, hd, n_slots, lookup_ref, counts_ref, q_ref, do_ref, kv_ref,
    att_ref, dq_ref, g_ref,
    kv_t, k_n, v_n, dk_acc, dv_acc, e_s, ds_s,
):
    cols = n_heads * hd
    wide = n_heads * BLK
    ext = kv_ref.shape[1] // BLK

    @pl.loop(0, ext, unroll=8)
    def _(i):
        both = kv_ref[:, pl.ds(pl.multiple_of(i * BLK, BLK), BLK)]
        kv_t[i] = both
        k_n[i] = both[:cols].T
        v_n[i] = both[cols:].T
        zero = jnp.zeros((BLK, cols), F32)
        dk_acc[i] = zero
        dv_acc[i] = zero

    def diagonal(parts):
        rows = []
        for h in range(n_heads):
            zero = jnp.zeros((hd, BLK), BF16)
            rows.append(
                jnp.concatenate([parts[h] if g == h else zero for g in range(n_heads)], axis=1)
            )
        return jnp.concatenate(rows, axis=0)

    def of_head(value, h):
        return value[h * hd : (h + 1) * hd, h * BLK : (h + 1) * BLK]

    def scores(b, e_s):
        at = pl.ds(pl.multiple_of(b * BLK, BLK), BLK)
        q_t = q_ref[:, at]
        do_t = do_ref[:, at]
        slots = [lookup_ref[b, j] for j in range(n_slots)]
        count = counts_ref[b]
        q_diag = diagonal([q_t[h * hd : (h + 1) * hd] for h in range(n_heads)])
        total = jnp.zeros((1, wide), F32)
        for j in range(n_slots):
            raised = jnp.exp2(dot(k_n[slots[j]], q_diag))
            raised = raised * jnp.where(j < count, 1.0, 0.0)
            total = total + jnp.sum(raised, axis=0, keepdims=True)
            e_s[j * BLK : (j + 1) * BLK, :] = raised.astype(BF16)
        return at, q_t, do_t, slots, q_diag, total

    def middle(state, e_s):
        at, q_t, do_t, slots, q_diag, total = state
        values_t = jnp.concatenate([kv_t[s][cols:] for s in slots], axis=1)
        keys_t = jnp.concatenate([kv_t[s][:cols] for s in slots], axis=1)
        out = dot(values_t, e_s[...])
        share = 1.0 / total
        att, scaled, inner = [], [], []
        for h in range(n_heads):
            share_h = share[:, h * BLK : (h + 1) * BLK]
            att_h = of_head(out, h) * share_h
            do_h = do_t[h * hd : (h + 1) * hd].astype(F32) * share_h
            att.append(att_h)
            scaled.append(do_h.astype(BF16))
            inner.append(jnp.sum(att_h * do_h, axis=0, keepdims=True))
        att_ref[:, at] = jnp.concatenate(att, axis=0).astype(BF16)
        inner = jnp.concatenate(inner, axis=1)
        do_diag = diagonal(scaled)
        q_rows = q_diag.T
        do_rows = do_diag.T
        return at, slots, keys_t, do_diag, q_rows, do_rows, inner

    def backward(state, e_s, ds_s):
        at, slots, keys_t, do_diag, q_rows, do_rows, inner = state
        for j in range(n_slots):
            rows = slice(j * BLK, (j + 1) * BLK)
            e = e_s[rows, :]
            d = e.astype(F32) * (dot(v_n[slots[j]], do_diag) - inner)
            d = d.astype(BF16)
            ds_s[rows, :] = d
            dk_acc[slots[j]] += dot(d, q_rows)
            dv_acc[slots[j]] += dot(e, do_rows)
        dq = dot(keys_t, ds_s[...])
        dq = jnp.concatenate([of_head(dq, h) for h in range(n_heads)], axis=0)
        dq_ref[:, at] = (dq * SCORE_SCALE).astype(dq_ref.dtype)

    @pl.loop(0, q_ref.shape[1] // BLK, step=2)
    def _(b):
        one = scores(b, e_s.at[0])
        two = scores(b + 1, e_s.at[1])
        one = middle(one, e_s.at[0])
        two = middle(two, e_s.at[1])
        backward(one, e_s.at[0], ds_s.at[0])
        backward(two, e_s.at[1], ds_s.at[1])

    @pl.loop(0, ext, unroll=8)
    def _(i):
        at = pl.ds(pl.multiple_of(i * BLK, BLK), BLK)
        g_ref[:cols, at] = (dk_acc[i] * math.log(2.0)).T.astype(g_ref.dtype)
        g_ref[cols:, at] = dv_acc[i].T.astype(g_ref.dtype)


def attention(lookup, counts, q_t, do_t, kv_ext, hd):
    cols, rows = q_t.shape
    n_heads = cols // hd
    n_slots = lookup.shape[1]
    ext = kv_ext.shape[1] // BLK
    smem = pl.BlockSpec(memory_space=pltpu.SMEM)
    vmem = pl.BlockSpec(memory_space=pltpu.VMEM)
    shape = jax.ShapeDtypeStruct
    return pl.pallas_call(
        functools.partial(attention_kernel, n_heads, hd, n_slots),
        out_shape=(
            shape((cols, rows), BF16),
            shape((cols, rows), BF16),
            shape(kv_ext.shape, BF16),
        ),
        in_specs=[smem, smem] + [vmem] * 3,
        out_specs=(vmem,) * 3,
        scratch_shapes=[
            pltpu.VMEM((ext, 2 * cols, BLK), BF16),
            pltpu.VMEM((ext, BLK, cols), BF16),
            pltpu.VMEM((ext, BLK, cols), BF16),
            pltpu.VMEM((ext, BLK, cols), F32),
            pltpu.VMEM((ext, BLK, cols), F32),
            pltpu.VMEM((2, n_slots * BLK, n_heads * BLK), BF16),
            pltpu.VMEM((2, n_slots * BLK, n_heads * BLK), BF16),
        ],
        compiler_params=pltpu.CompilerParams(vmem_limit_bytes=52 * 1024 * 1024),
    )(lookup, counts, q_t, do_t, kv_ext)


def sender(src, dst, send_sem, recv_sem, target):
    copy = pltpu.make_async_remote_copy(
        src_ref=src, dst_ref=dst, send_sem=send_sem, recv_sem=recv_sem,
        device_id=target, device_id_type=MESH,
    )
    copy.start()
    return copy


def gather_kernel(
    n_slab, n_head, normed_ref, d_att_ref, ext_ref, d_heads_ref,
    h_send, h_recv, x_send, x_recv, c_send, c_recv, f_send, f_recv, a_send, a_recv,
):
    slab, head = lax.axis_index("slab"), lax.axis_index("head")
    up, down = lax.rem(slab + 1, n_slab), lax.rem(slab + n_slab - 1, n_slab)
    core = (head // 2) * 2 + 1 - lax.rem(head, 2)
    across = lax.rem(head + 2, n_head)
    rows = normed_ref.shape[0]
    cols = d_heads_ref.shape[0]

    barrier = pltpu.get_barrier_semaphore()
    for s in (up, down):
        pl.semaphore_signal(barrier, inc=1, device_id=(s, head), device_id_type=MESH)
    for k in range(1, n_head):
        pl.semaphore_signal(
            barrier, inc=1, device_id=(slab, lax.rem(head + k, n_head)), device_id_type=MESH
        )
    pl.semaphore_wait(barrier, n_head + 1)

    n_chunks = h_send.shape[1]
    size = rows // n_chunks

    def at(t, h, c):
        return ext_ref.at[t, h, pl.ds(c * size, size)]

    def spread(t, c, src):
        return [
            sender(src, at(t, head, c), x_send.at[t, c], x_recv.at[t, c], (slab, across)),
            sender(src, at(t, head, c), c_send.at[t, c], c_recv.at[t, c], (slab, core)),
        ]

    def forward(t, c):
        return sender(
            at(t, across, c), at(t, across, c), f_send.at[t, c], f_recv.at[t, c], (slab, core)
        )

    own, low, high, to_up, to_down, ahead = [], [], [], [], [], []
    for c in range(n_chunks):
        src = normed_ref.at[pl.ds(c * size, size)]
        to_up.append(sender(src, at(0, head, c), h_send.at[0, c], h_recv.at[0, c], (up, head)))
        to_down.append(
            sender(src, at(2, head, c), h_send.at[1, c], h_recv.at[1, c], (down, head))
        )
        own.append(spread(1, c, src))
    mine = pl.ds(pl.multiple_of(head * rows, 128), rows)
    d_heads_ref[:, mine] = d_att_ref[pl.ds(pl.multiple_of(head * cols, 16), cols), :]
    ext_ref[1, head] = normed_ref[...]
    for c in range(n_chunks):
        to_up[c].wait_recv()
        low.append(spread(0, c, at(0, head, c)))
        to_down[c].wait_recv()
        high.append(spread(2, c, at(2, head, c)))
        own[c][0].wait_recv()
        ahead.append(forward(1, c))
    sent = []
    for k in range(1, n_head):
        h = lax.rem(head + k, n_head)
        sent.append(
            sender(
                d_att_ref.at[pl.ds(pl.multiple_of(h * cols, 16), cols)],
                d_heads_ref.at[:, mine],
                a_send.at[k], a_recv.at[k], (slab, h),
            )
        )
    for c in range(n_chunks):
        low[c][0].wait_recv()
        ahead.append(forward(0, c))
        high[c][0].wait_recv()
        ahead.append(forward(2, c))
    for c in range(n_chunks):
        for copy in (to_up[c], to_down[c], own[c][0], low[c][0], high[c][0]):
            copy.wait_send()
        for copy in (own[c][1], low[c][1], high[c][1]):
            copy.wait()
    for copy in (*ahead, *sent):
        copy.wait()


def gather_slabs(normed, d_attended):
    n_slab, n_head = lax.axis_size("slab"), lax.axis_size("head")
    rows, width = normed.shape
    cols = width // n_head
    vmem = pl.BlockSpec(memory_space=pltpu.VMEM)
    shape = jax.ShapeDtypeStruct
    dma = pltpu.SemaphoreType.DMA
    return pl.pallas_call(
        functools.partial(gather_kernel, n_slab, n_head),
        out_shape=(
            shape((3, n_head, rows, width), BF16),
            shape((cols, n_head * rows), BF16),
        ),
        in_specs=[vmem] * 2,
        out_specs=(vmem,) * 2,
        scratch_shapes=[dma((2, 4))] * 2 + [dma((3, 4))] * 6 + [dma((n_head,))] * 2,
        compiler_params=pltpu.CompilerParams(
            collective_id=1, has_side_effects=True, vmem_limit_bytes=32 * 1024 * 1024
        ),
    )(normed, d_attended)


def sums_kernel(
    n_slab, n_head, att_ref, cot_ref, low_ref, own_ref, high_ref, qkv_ref, w_ref, gain_ref,
    attended_ref, dn_ref, d_qkv_ref, d_out_ref, d_gain_ref,
    pair_in, pair_out, x_in, rim_out, rim_in,
    out_part, heads_in, full, slabs_in, chunk, done_out, gain_part, gains_in, outs_in,
    p_send, p_recv, x_send, x_recv, r_send, r_recv, t_send, t_recv,
    send_a, recv_a, send_b, recv_b, send_c, recv_c, send_d, recv_d, send_e, recv_e,
):
    slab, head = lax.axis_index("slab"), lax.axis_index("head")
    up, down = lax.rem(slab + 1, n_slab), lax.rem(slab + n_slab - 1, n_slab)
    core = (head // 2) * 2 + 1 - lax.rem(head, 2)
    across = lax.rem(head + 2, n_head)
    corner = lax.rem(core + 2, n_head)
    rows_q = qkv_ref.shape[0]
    rows_o = att_ref.shape[0]
    step = chunk.shape[0]
    rows = dn_ref.shape[0]
    parts = (low_ref, own_ref, high_ref)

    def other_heads():
        return [(k, lax.rem(head + k, n_head)) for k in range(1, n_head)]

    def other_slabs():
        return [(k, lax.rem(slab + k, n_slab)) for k in range(1, n_slab)]

    def of(h):
        return pl.ds(pl.multiple_of(h * rows, 128), rows)

    def out_rows(h):
        return pl.ds(pl.multiple_of(h * rows_o, 16), rows_o)

    barrier = pltpu.get_barrier_semaphore()
    for _, h in other_heads():
        pl.semaphore_signal(barrier, inc=1, device_id=(slab, h), device_id_type=MESH)
    for _, s in other_slabs():
        pl.semaphore_signal(barrier, inc=1, device_id=(s, head), device_id_type=MESH)
    pl.semaphore_wait(barrier, n_head + n_slab - 2)

    n_chunks = x_send.shape[1]
    size = rows // n_chunks

    def span(c):
        return pl.ds(c * size, size)

    def of_chunk(h, c):
        return pl.ds(pl.multiple_of(h * rows + c * size, 128), size)

    def send_pair(t, c, i):
        return sender(
            parts[t].at[of_chunk((corner, core)[i], c)], pair_in.at[t, i, span(c)],
            p_send.at[t, i, c], p_recv.at[t, i, c], (slab, core),
        )

    def pair_sum(t, c, copy):
        copy.wait()
        pair_out[t, span(c)] = (
            parts[t][of_chunk(across, c), :].astype(F32) + pair_in[t, 0, span(c)].astype(F32)
        ).astype(BF16)
        return sender(
            pair_out.at[t, span(c)], x_in.at[t, span(c)],
            x_send.at[t, c], x_recv.at[t, c], (slab, across),
        )

    def whole_sum(t, c):
        return (
            parts[t][of_chunk(head, c), :].astype(F32)
            + pair_in[t, 1, span(c)].astype(F32)
            + x_in[t, span(c)].astype(F32)
        )

    def rim(i, t, c, target):
        pairs[t, c, 1].wait()
        crossing[t, c].wait()
        rim_out[i, span(c)] = whole_sum(t, c).astype(BF16)
        return sender(
            rim_out.at[i, span(c)], rim_in.at[i, span(c)],
            r_send.at[i, c], r_recv.at[i, c], (target, head),
        )

    sent = []
    for k, h in other_heads():
        sent.append(
            sender(
                att_ref.at[:, of(h)], attended_ref.at[out_rows(head)],
                t_send.at[k], t_recv.at[k], (slab, h),
            )
        )
    pairs, crossing, rims = {}, {}, []
    order = [(t, c) for c in range(n_chunks) for t in (0, 2)]
    order += [(1, c) for c in range(n_chunks)]
    for i in range(2):
        for t, c in order:
            pairs[t, c, i] = send_pair(t, c, i)
    attended_ref[out_rows(head), :] = att_ref[:, of(head)]
    full[:rows_q, :] = qkv_ref[...]
    if full.shape[0] > rows_q + rows_o:
        full[rows_q + rows_o :, :] = jnp.zeros(
            (full.shape[0] - rows_q - rows_o, full.shape[1]), BF16
        )
    half = len(order) // 3
    for t, c in order[:half]:
        crossing[t, c] = pair_sum(t, c, pairs[t, c, 0])

    for copy in sent:
        copy.wait()
    out_part[...] = dot(attended_ref[...], cot_ref[...]).astype(BF16)
    sent = []
    for k, h in other_heads():
        sent.append(
            sender(
                out_part.at[out_rows(h)], heads_in.at[k], send_a.at[k], recv_a.at[k], (slab, h)
            )
        )
    for t, c in order[half:]:
        crossing[t, c] = pair_sum(t, c, pairs[t, c, 0])
    for t, c in order[:half]:
        rims.append(rim(t // 2, t, c, (down, None, up)[t]))

    total = out_part[out_rows(head), :].astype(F32)
    for k in range(1, n_head):
        sent[k - 1].wait()
        total += heads_in[k].astype(F32)
    full[rows_q : rows_q + rows_o, :] = total.astype(BF16)
    sent = []
    for k, s in other_slabs():
        part = pl.ds(pl.multiple_of(s * step, 16), step)
        sent.append(sender(full.at[part], slabs_in.at[k], send_b.at[k], recv_b.at[k], (s, head)))
    for t, c in order[half : 2 * half]:
        rims.append(rim(t // 2, t, c, (down, None, up)[t]))

    mine = pl.ds(pl.multiple_of(slab * step, 16), step)
    total = full[mine, :].astype(F32)
    for k in range(1, n_slab):
        sent[k - 1].wait()
        total += slabs_in[k].astype(F32)
    chunk[...] = total.astype(BF16)
    sent = []
    for k, s in other_slabs():
        sent.append(sender(chunk, done_out.at[mine], send_c.at[k], recv_c.at[k], (s, head)))
    done_out[mine, :] = chunk[...]
    for t, c in order[2 * half :]:
        pairs[t, c, 1].wait()
        crossing[t, c].wait()
        dn_ref[span(c), :] = whole_sum(t, c)
    for copy in sent:
        copy.wait()

    own = done_out.at[pl.ds(rows_q, rows_o)]
    sent = []
    for k, h in other_heads():
        sent.append(sender(own, outs_in.at[k], send_d.at[k], recv_d.at[k], (slab, h)))
    summed = done_out[:rows_q, :].astype(F32)
    part = jnp.sum(summed * w_ref[...].astype(F32), axis=0, keepdims=True) / gain_ref[...]
    gain_part[...] = jnp.broadcast_to(part, gain_part.shape)
    for k, h in other_heads():
        sent.append(sender(gain_part, gains_in.at[k], send_e.at[k], recv_e.at[k], (slab, h)))
    d_qkv_ref[...] = summed
    d_out_ref[out_rows(head), :] = done_out[rows_q : rows_q + rows_o, :].astype(F32)
    for copy in rims:
        copy.wait()
    dn_ref[...] += rim_in[0].astype(F32) + rim_in[1].astype(F32)
    for copy in sent:
        copy.wait()
    gains_in[0] = gain_part[...]
    total = jnp.zeros(gain_part.shape, F32)
    for h in range(n_head):
        total += gains_in[lax.rem(head + n_head - h, n_head)]
    for k in range(1, n_head):
        source = lax.rem(head + n_head - k, n_head)
        d_out_ref[out_rows(source), :] = outs_in[k].astype(F32)
    d_gain_ref[...] = total


def grad_sums(att_t, cotangent, low, own, high, qkv_part, w_t, gain):
    n_slab, n_head = lax.axis_size("slab"), lax.axis_size("head")
    rows_q, width = qkv_part.shape
    rows_o = att_t.shape[0]
    rows = cotangent.shape[0]
    step = -(-(rows_q + rows_o) // (16 * n_slab)) * 16
    vmem = pl.BlockSpec(memory_space=pltpu.VMEM)
    shape = jax.ShapeDtypeStruct
    dma = pltpu.SemaphoreType.DMA
    return pl.pallas_call(
        functools.partial(sums_kernel, n_slab, n_head),
        out_shape=(
            shape((width, rows), BF16),
            shape((rows, width), F32),
            shape((rows_q, width), F32),
            shape((width, width), F32),
            shape((8, width), F32),
        ),
        in_specs=[vmem] * 8,
        out_specs=(vmem,) * 5,
        scratch_shapes=[
            pltpu.VMEM((3, 2, rows, width), BF16),
            pltpu.VMEM((3, rows, width), BF16),
            pltpu.VMEM((3, rows, width), BF16),
            pltpu.VMEM((2, rows, width), BF16),
            pltpu.VMEM((2, rows, width), BF16),
            pltpu.VMEM((width, width), BF16),
            pltpu.VMEM((n_head, rows_o, width), BF16),
            pltpu.VMEM((n_slab * step, width), BF16),
            pltpu.VMEM((n_slab, step, width), BF16),
            pltpu.VMEM((step, width), BF16),
            pltpu.VMEM((n_slab * step, width), BF16),
            pltpu.VMEM((8, width), F32),
            pltpu.VMEM((n_head, 8, width), F32),
            pltpu.VMEM((n_head, rows_o, width), BF16),
        ]
        + [dma((3, 2, 4))] * 2 + [dma((3, 4))] * 2 + [dma((2, 4))] * 2 + [dma((n_head,))] * 4
        + [dma((n_slab,))] * 4 + [dma((n_head,))] * 4,
        compiler_params=pltpu.CompilerParams(
            collective_id=0, has_side_effects=True, vmem_limit_bytes=48 * 1024 * 1024
        ),
    )(att_t, cotangent, low, own, high, qkv_part, w_t, gain)


def over_rows(a, b):
    return lax.dot_general(a, b, (((0,), (0,)), ((), ())), preferred_element_type=F32)


def over_width(a, b):
    return lax.dot_general(a, b, (((1,), (1,)), ((), ())), preferred_element_type=F32)


def local(tokens, norm_gain, w_qkv, w_out, cotangent, neighbours, counts):
    width = tokens.shape[1]
    hd = width // HEADS
    n_head, n_slab = lax.axis_size("head"), lax.axis_size("slab")
    cols = width // n_head
    here = HEADS // n_head
    head_index, slab_index = lax.axis_index("head"), lax.axis_index("slab")
    slab_blocks = neighbours.shape[0]
    slab_rows = slab_blocks * BLK
    tok = tokens.astype(F32)
    inverse = lax.rsqrt(jnp.mean(tok * tok, -1, keepdims=True) + norm_eps)
    normed = (tok * inverse * norm_gain).astype(BF16)
    w_here = lax.dynamic_slice_in_dim(w_qkv, head_index * cols, cols, 2)
    w_t = w_here.transpose(0, 2, 1).reshape(3 * cols, width)
    d_attended = over_width(w_out, cotangent).astype(BF16)
    gathered, d_heads = gather_slabs(normed, d_attended)
    gathered = gathered.reshape(3 * slab_rows, width)
    own_rows = gathered[slab_rows : 2 * slab_rows]

    floor = 0.7 * math.sqrt(hd)

    def unit_of(projected):
        by_head = projected.reshape(here, hd, -1)
        length = jnp.sqrt(jnp.sum(by_head * by_head, 1, keepdims=True))
        divisor = jnp.maximum(length, floor)
        return by_head / divisor, divisor, length > floor

    def unit_back(parts, grad):
        unit, divisor, active = parts
        along = grad.astype(F32).reshape(unit.shape)
        inner = jnp.sum(unit * along, 1, keepdims=True)
        result = (along - jnp.where(active, unit * inner, 0.0)) / divisor
        return result.reshape(grad.shape).astype(BF16)

    q_parts = unit_of(over_width(w_t[:cols], own_rows))
    kv = over_width(w_t[cols:], gathered)
    k_parts = unit_of(kv[:cols])
    q_t = (q_parts[0] * (SCORE_SCALE * LOG2E)).reshape(cols, slab_rows).astype(BF16)
    kv_ext = jnp.concatenate(
        [k_parts[0].reshape(cols, 3 * slab_rows).astype(BF16), kv[cols:].astype(BF16)], 0
    )
    lookup = (neighbours - slab_index * slab_blocks + REACH) % (slab_blocks * n_slab)
    att_t, dq_t, g_kv = attention(lookup, counts, q_t, d_heads, kv_ext, hd)

    d_q = unit_back(q_parts, dq_t)
    d_kv = jnp.concatenate([unit_back(k_parts, g_kv[:cols]), g_kv[cols:]], 0)
    low, high = d_kv[:, :slab_rows], d_kv[:, 2 * slab_rows :]
    own = jnp.concatenate([d_q, d_kv[:, slab_rows : 2 * slab_rows]], 0)
    qkv_part = jnp.concatenate([dot(d_q, own_rows), dot(d_kv, gathered)], 0).astype(BF16)
    attended, d_normed, d_w, d_w_out, d_gain = grad_sums(
        att_t,
        cotangent,
        over_rows(low, w_t[cols:]).astype(BF16),
        over_rows(own, w_t).astype(BF16),
        over_rows(high, w_t[cols:]).astype(BF16),
        qkv_part,
        w_t,
        norm_gain.reshape(1, width),
    )
    output = (tok + over_rows(attended, w_out)).astype(BF16)
    d_w_qkv = d_w.reshape(3, cols, width).transpose(0, 2, 1)
    scaled = d_normed * norm_gain
    d_tokens = (
        cotangent.astype(F32)
        + inverse * scaled
        - tok * inverse**3 * jnp.mean(scaled * tok, -1, keepdims=True)
    )
    return (output, d_tokens.astype(BF16), d_w_qkv, d_w_out, d_gain[0])


def solution(mesh):
    placed = (
        P(("slab", "head"), None),
        P(),
        P(),
        P(),
        P(("slab", "head"), None),
        P("slab", None),
        P("slab"),
    )
    return jax.shard_map(
        local,
        mesh=mesh,
        in_specs=placed,
        out_specs=(
            P(("slab", "head"), None),
            P(("slab", "head"), None),
            P(None, None, "head"),
            P(),
            P(),
        ),
        check_vma=False,
    )
```
